256 devices in a mesh: leaf: 256 (over y, x, z, core).
Axes of the slice: x: 4, y: 4, z: 8, core: 2. Of those that a mesh axis runs over, the one named last changes fastest.
Arguments:
- positions: float32 [3, 2097152], P(None, 'leaf'), may hold values from -5 to 5, as said below
- charges: float32 [32, 2097152], P(None, 'leaf'), may hold values from -0.3 to 0.3
- bases: float32 [16384, 128, 128], P('leaf'), may hold values from -0.5 to 0.5
- transfer: float32 [2, 128, 128], replicated, may hold values from -0.4375 to 0.4375
- unit_nodes: float32 [3, 128], replicated, may hold values from -3 to 3
- near_list: int32 [16384, 8], P('leaf'), may hold values from 0 to 16383, as said below
- near_count: int32 [16384], P('leaf'), may hold values from 1 to 8, as said below
- far_list: int32 [16384, 8], P('leaf'), may hold values from 0 to 16383, as said below
Outputs:
- potential: float32 [32, 2097152], P(None, 'leaf')
The draws below stay inside these ranges and needn't reach their ends.
Inputs may be any that keep to these rules, and one draw needn't show every extreme that they name: near_list[l, 0] = l; the entries of a row are distinct leaves within 32 of l. Slots 0 to near_count[l] - 1 of row l of near_list are used. `far_list`: the entries of a row are distinct leaves within 32 of l, none of them in the same row of near_list. `positions`: the coordinates lie within this range.
All inputs are finite; a program needn't handle non-finite values.
Results may differ from the reference program's by a relative error of at most 0.0003.
Values sent between devices are 32-bit elements; how exact they have to be, the bound alone decides.
A program may use at most 128 MiB of HBM per device.

```python
import jax
import jax.numpy as jnp
from jax import lax

P_SIZE = 128
K = 128
RHS = 32
NEAR = 8
FAR = 8
LEAF_DEV = 64
REACH = 32
LEAVES = 16384
PANELS = 2097152


def window_order(key):
    span_size = 2 * REACH + 1
    offsets = jnp.arange(span_size, dtype=jnp.int32) - REACH
    leaf_ids = jnp.arange(LEAVES, dtype=jnp.int32)
    targets = leaf_ids[:, None] + offsets[None, :]
    noise = jax.random.randint(key, (LEAVES, span_size), 0, 1 << 20, dtype=jnp.int32)
    scores = noise * span_size + offsets[None, :] + REACH
    outside = (targets < 0) | (targets >= LEAVES)
    scores = jnp.where(outside, scores + (1 << 30), scores)
    scores = jnp.where(offsets[None, :] == 0, -1, scores)
    order = jnp.argsort(scores, axis=1, stable=True)
    return jnp.take_along_axis(targets, order, axis=1).astype(jnp.int32)


def draw_near_list(key, part):
    chosen = window_order(key)
    return chosen[:, :NEAR]


def draw_far_list(key, part):
    chosen = window_order(key)
    return chosen[:, NEAR:NEAR + FAR]


def draw_near_count(key, part):
    key = jax.random.fold_in(key, 3)
    first_key, second_key, third_key = jax.random.split(key, 3)
    device_total = LEAVES // LEAF_DEV
    ceiling = jax.random.randint(first_key, (device_total,), 2, NEAR + 1, dtype=jnp.int32)
    busiest = jax.random.randint(second_key, (), 0, device_total, dtype=jnp.int32)
    ceiling = jnp.where(jnp.arange(device_total, dtype=jnp.int32) == busiest, NEAR, ceiling)
    per_leaf = jnp.repeat(ceiling, LEAF_DEV, total_repeat_length=LEAVES)
    lower = (per_leaf + 1) // 2
    counts = jax.random.randint(third_key, (LEAVES,), lower, per_leaf + 1, dtype=jnp.int32)
    leading = jnp.arange(LEAVES, dtype=jnp.int32) % LEAF_DEV == 0
    return jnp.where(leading, per_leaf, counts).astype(jnp.int32)


def draw_positions(key, part):
    key = jax.random.fold_in(key, 4)
    leaf_index = (jnp.arange(LEAVES * P_SIZE, dtype=jnp.int32) // P_SIZE).astype(jnp.float32)
    turn = 0.1 * leaf_index
    center = jnp.stack([2.5 * jnp.cos(turn), 2.5 * jnp.sin(turn), 2.0 * jnp.sin(0.0031 * leaf_index)])
    spread = jax.random.truncated_normal(key, -2.0, 2.0, (3, LEAVES * P_SIZE), jnp.float32)
    return center + spread


def levels(rng, dims, cuts, least, high):
    def one(dim, shards_of):
        steps = jax.random.uniform(jax.random.fold_in(jax.random.fold_in(rng, 6), dim), (shards_of,), jnp.float32, least / len(cuts), high / len(cuts))
        return jnp.repeat(jnp.exp(steps), dims[dim] // shards_of).reshape((-1,) + (1,) * (len(dims) - dim - 1))

    gain = one(*cuts[0])
    for cut in cuts[1:]:
        gain = gain * one(*cut)
    return gain


def bell_draw(stream_key, shape, width, most, cuts=(), kind=jnp.bfloat16):
    loudness = levels(stream_key, shape, cuts, -0.22, 0.18) if cuts else 1.0
    array = jax.random.normal(stream_key, shape, jnp.float32) * width * loudness
    return jnp.minimum(jnp.maximum(array, -most), most).astype(kind)


def setup_inputs(seed: int = 0) -> dict:
    seeds = jax.random.split(jax.random.key(seed), 9)
    return {
        "positions": draw_positions(jax.random.fold_in(seeds[8], 71), 0),
        "charges": bell_draw(seeds[1], (RHS, PANELS), 0.05, 0.3, ((1, 256),), jnp.float32),
        "bases": bell_draw(seeds[2], (LEAVES, P_SIZE, K), P_SIZE ** -0.5, 0.5, ((0, 256),), jnp.float32),
        "transfer": bell_draw(seeds[3], (2, K, K), (K * 99 // 70) ** -0.5, 0.4375, (), jnp.float32),
        "unit_nodes": jnp.clip(jax.random.uniform(seeds[4], (3, K), jnp.float32, -3.0, 3.0), -3.0, 3.0),
        "near_list": draw_near_list(jax.random.fold_in(seeds[8], 71), 0),
        "near_count": draw_near_count(jax.random.fold_in(seeds[8], 71), 0),
        "far_list": draw_far_list(jax.random.fold_in(seeds[8], 71), 0),
    }


DELTA_SQ = 0.0625
RADIUS = 0.4
GROWTH = 1.26
FULL = lax.Precision.HIGHEST

def kernel_block(targets, sources):
    spacing = targets[..., 0, :, None] - sources[..., 0, None, :]
    dist_sq = spacing * spacing
    for axis_num in range(1, 3):
        spacing = targets[..., axis_num, :, None] - sources[..., axis_num, None, :]
        dist_sq = dist_sq + spacing * spacing
    return lax.rsqrt(dist_sq + DELTA_SQ)

def node_points(centers, height, unit_nodes):
    return centers[:, :, None] + RADIUS * GROWTH ** height * unit_nodes[None]

def couple_blocks(target_centers, source_centers, source_coeffs, height, unit_nodes):
    count_all = target_centers.shape[0]
    block_size = min(count_all, 64)

    def one_block(inputs):
        target_part, source_part, coeff_part = inputs
        kernel_tile = kernel_block(node_points(target_part, height, unit_nodes), node_points(source_part, height, unit_nodes))
        return jnp.einsum('cab,crb->cra', kernel_tile, coeff_part, precision=FULL)
    result = lax.map(one_block, (target_centers.reshape(count_all // block_size, block_size, 3), source_centers.reshape(count_all // block_size, block_size, 3), source_coeffs.reshape(count_all // block_size, block_size, RHS, K)))
    return result.reshape(count_all, RHS, K)

def reference(positions, charges, bases, transfer, unit_nodes, near_list, near_count, far_list):
    height_total = LEAVES.bit_length() - 1
    points = positions.reshape(3, LEAVES, P_SIZE)
    charge_blocks = charges.reshape(RHS, LEAVES, P_SIZE)
    upward = [jnp.einsum('rlp,lpk->lrk', charge_blocks, bases, precision=FULL)]
    centers_up = [lax.optimization_barrier(jnp.mean(points, axis=2)).T]
    for height in range(height_total):
        paired = upward[-1].reshape(-1, 2, RHS, K)
        upward.append(jnp.einsum('crk,kj->crj', paired[:, 0], transfer[0], precision=FULL) + jnp.einsum('crk,kj->crj', paired[:, 1], transfer[1], precision=FULL))
        center_pairs = centers_up[-1].reshape(-1, 2, 3)
        centers_up.append((center_pairs[:, 0] + center_pairs[:, 1]) * 0.5)
    down_field = jnp.zeros((1, RHS, K), jnp.float32)
    for height in range(height_total - 1, -1, -1):
        left_field = jnp.einsum('crk,jk->crj', down_field, transfer[0], precision=FULL)
        right_field = jnp.einsum('crk,jk->crj', down_field, transfer[1], precision=FULL)
        children = jnp.stack([left_field, right_field], axis=1).reshape(-1, RHS, K)
        if height >= 1:
            swapped = upward[height].reshape(-1, 2, RHS, K)[:, ::-1].reshape(-1, RHS, K)
            partner_centers = centers_up[height].reshape(-1, 2, 3)[:, ::-1].reshape(-1, 3)
            children = children + couple_blocks(centers_up[height], partner_centers, swapped, height, unit_nodes)
        else:
            for slot_num in range(FAR):
                chosen = far_list[:, slot_num]
                children = children + couple_blocks(centers_up[0], jnp.take(centers_up[0], chosen, axis=0), jnp.take(upward[0], chosen, axis=0), 0, unit_nodes)
        down_field = children
    far_part = jnp.einsum('lrk,lpk->rlp', down_field, bases, precision=FULL)
    block_size = min(LEAVES, 64)
    groups = LEAVES // block_size
    target_points = points.transpose(1, 0, 2).reshape(groups, block_size, 3, P_SIZE)

    def near_group(inputs):
        group_targets, group_lists, group_counts = inputs
        running = jnp.zeros((RHS, block_size, P_SIZE), jnp.float32)
        for slot_num in range(NEAR):
            chosen = group_lists[:, slot_num]
            source_points = jnp.take(points, chosen, axis=1).transpose(1, 0, 2)
            kernel_tile = kernel_block(group_targets, source_points)
            live_mask = (slot_num < group_counts).astype(jnp.float32)
            running = running + jnp.einsum('lab,rlb->rla', kernel_tile * live_mask[:, None, None], jnp.take(charge_blocks, chosen, axis=1), precision=FULL)
        return running
    near_blocks = lax.map(near_group, (target_points, near_list.reshape(groups, block_size, NEAR), near_count.reshape(groups, block_size)))
    near_part = near_blocks.transpose(1, 0, 2, 3).reshape(RHS, LEAVES, P_SIZE)
    return (far_part + near_part).reshape(RHS, LEAVES * P_SIZE)
```

```python
import functools

import jax
import jax.numpy as jnp
from jax import lax
from jax.experimental import pallas as pl
from jax.experimental.pallas import tpu as pltpu
from jax.sharding import PartitionSpec as P

DELTA_SQ = 0.0625
RADIUS = 0.4
GROWTH = 1.26
F32, BF16 = jnp.float32, jnp.bfloat16
MESH = pl.DeviceIdType.MESH
NT = (((1,), (1,)), ((), ()))
FEATS = 48


def dot(a, b):
    return jnp.dot(a, b, preferred_element_type=F32)


def dot_nt(a, b):
    return lax.dot_general(a, b, NT, preferred_element_type=F32)


def halves(x):
    hi = x.astype(BF16)
    return hi, (x - hi.astype(F32)).astype(BF16)


def thirds(x):
    a = x.astype(BF16).astype(F32)
    rest = x - a
    b = rest.astype(BF16).astype(F32)
    return a, b, rest - b


def stacked(x):
    hi, lo = halves(x)
    return jnp.concatenate([hi, lo], axis=0)


def target_feats(y):
    a, b, c = thirds(y)
    return jnp.concatenate([a, a, a, b, b, c], axis=0).astype(BF16)


def source_feats(x):
    a, b, c = thirds(x)
    return jnp.concatenate([a, b, c, a, b, a], axis=0).T.astype(BF16)


def row_ids():
    return lax.broadcasted_iota(jnp.int32, (8, 128), 0)


def rows3(ref, lanes):
    rows = row_ids()
    x = jnp.where(rows == 0, ref[0:1, lanes], 0.0)
    x = jnp.where(rows == 1, ref[1:2, lanes], x)
    return jnp.where(rows == 2, ref[2:3, lanes], x)


def as_source(x):
    rows = row_ids()
    norm = jnp.sum(x * x, axis=0, keepdims=True)
    return jnp.where(rows == 3, 1.0, jnp.where(rows == 4, norm, -2.0 * x))


def as_target(y, scale):
    rows = row_ids()
    norm = jnp.sum(y * y, axis=0, keepdims=True)
    return jnp.where(rows == 3, norm + DELTA_SQ, jnp.where(rows == 4, scale * scale, scale * y))


def as_link(gap, units, scale):
    rest = jnp.sum(gap * (gap + (2.0 * scale) * units), axis=0, keepdims=True)
    return jnp.where(row_ids() == 3, rest, scale * gap)


def fold(r):
    m, n = r.shape[0] // 2, r.shape[1] // 2
    return r[:m, :n] + (r[:m, n:] + r[m:, :n]) + r[m:, n:]


def tiles(left, right, extra=None):
    dist_sq = dot(left, right)
    hi, lo = halves(lax.rsqrt(dist_sq if extra is None else dist_sq + extra))
    return [
        jnp.concatenate([hi[:, i : i + 128], lo[:, i : i + 128]], axis=1)
        for i in range(0, right.shape[1], 128)
    ]


def tree_kernel(
    n,
    pos_in,
    chg_in,
    bases_in,
    transfer_in,
    unit_in,
    far,
    out,
    halo_pos_l,
    halo_pos_r,
    halo_chg_l,
    halo_chg_r,
    pos,
    chg,
    bases,
    transfer,
    unit,
    wide_u,
    wide_w,
    wide_c,
    ulev,
    clev,
    vlev,
    vfar,
    up_mat,
    down_mat,
    unit_left,
    unit_gaps,
    cmsg,
    snd,
    rcv,
    send_sem,
    recv_sem,
    load_sem,
):
    me = lax.axis_index("leaf")
    leaf_dev = bases_in.shape[0]
    half = leaf_dev // 2
    local = leaf_dev.bit_length() - 1
    top = n.bit_length() - 1
    left, right = lax.rem(me + n - 1, n), lax.rem(me + 1, n)
    bits = [(me // (1 << b)) % 2 for b in range(top)]
    partners = [me + (1 << b) * (1 - 2 * bits[b]) for b in range(top)]
    offsets = [0] * (local + 1)
    for h in range(2, local + 1):
        offsets[h] = offsets[h - 1] + (leaf_dev >> (h - 1))

    group = 8
    parts = leaf_dev // group
    loads = [
        pltpu.make_async_copy(src, dst, load_sem.at[i])
        for i, (src, dst) in enumerate(
            [(transfer_in, transfer), (unit_in, unit), (pos_in, pos), (chg_in, chg)]
            + [(bases_in.at[pl.ds(j * group, group)], bases.at[pl.ds(j * group, group)]) for j in range(parts)]
        )
    ]
    for copy in loads:
        copy.start()
    barrier = pltpu.get_barrier_semaphore()
    for other in [left, right] + partners:
        pl.semaphore_signal(barrier, inc=1, device_id=(other,), device_id_type=MESH)
    pl.semaphore_wait(barrier, top + 2)
    for copy in loads[:4]:
        copy.wait()

    def remote(src, dst, which, device):
        return pltpu.make_async_remote_copy(
            src_ref=src,
            dst_ref=dst,
            send_sem=send_sem.at[which],
            recv_sem=recv_sem.at[which],
            device_id=(device,),
            device_id_type=MESH,
        )

    u_left = remote(wide_u.at[pl.ds(half, half)], wide_u.at[pl.ds(half + leaf_dev, half)], 0, left)
    u_right = remote(wide_u.at[pl.ds(leaf_dev, half)], wide_u.at[pl.ds(0, half)], 1, right)
    c_left = remote(cmsg.at[0], cmsg.at[2], 2, left)
    c_right = remote(cmsg.at[0], cmsg.at[1], 3, right)
    span = half * 128
    halo = [
        remote(chg.at[:, pl.ds(0, span)], halo_chg_r, 4, left),
        remote(chg.at[:, pl.ds(span, span)], halo_chg_l, 5, right),
        remote(pos.at[:, pl.ds(0, span)], halo_pos_r, 6, left),
        remote(pos.at[:, pl.ds(span, span)], halo_pos_l, 7, right),
    ]
    rounds = [remote(snd.at[b], rcv.at[b], 8 + b, partners[b]) for b in range(top)]

    t0, t1 = transfer[0], transfer[1]
    h0, l0 = halves(t0)
    h1, l1 = halves(t1)
    up_mat[...] = jnp.concatenate(
        [jnp.concatenate([h0, l0], axis=1), jnp.concatenate([h1, l1], axis=1)], axis=0
    )
    down_mat[...] = jnp.concatenate([h0, h1, l0, l1], axis=0)
    units = rows3(unit, slice(None))
    unit_left[...] = source_feats(as_source(units))
    columns = units.T
    gaps = [columns[:, c : c + 1] - units[c : c + 1, :] for c in range(3)]
    unit_gaps[...] = gaps[0] * gaps[0] + gaps[1] * gaps[1] + gaps[2] * gaps[2]
    lanes_id = lax.broadcasted_iota(jnp.int32, (8, 128), 1)

    def leaf_group(i, cols):
        loads[4 + i].wait()
        for k in range(group):
            l = i * group + k
            span_l = pl.ds(l * 128, 128)
            hi, lo = halves(bases[l])
            u = fold(dot(stacked(chg[:, span_l]), jnp.concatenate([hi, lo], axis=1)))
            wide_u[half + l] = u
            wide_w[half + l] = stacked(u)
            center = jnp.sum(rows3(pos, span_l), axis=1, keepdims=True) * (1.0 / 128)
            wide_c[half + l] = jnp.broadcast_to(center, (8, 128))
            cols = jnp.where(lanes_id == l, center, cols)
        return cols

    cols = jnp.zeros((8, 128), F32)
    for i in range(parts):
        cols = leaf_group(i, cols)
        if 2 * (i + 1) == parts:
            u_left.start()
    cmsg[0] = cols
    u_right.start()
    c_left.start()
    c_right.start()
    for copy in halo:
        copy.start()

    def merge(even, odd):
        m = even.shape[0]
        r = dot(stacked(jnp.concatenate([even, odd], axis=1)), up_mat[...])
        return r[:m, :128] + (r[:m, 128:] + r[m:, :128])

    def climb(src, first, dst, to, count):
        x = src[pl.ds(first, 2 * count)].reshape(count, 2, 32, 128)
        u = merge(x[:, 0].reshape(count * 32, 128), x[:, 1].reshape(count * 32, 128))
        dst[pl.ds(to, count)] = u.reshape(count, 32, 128)

    for h in range(1, local + 1):
        count = leaf_dev >> h
        src, first = (wide_u, half) if h == 1 else (ulev, offsets[h - 1])
        csrc = wide_c if h == 1 else clev
        c = csrc[pl.ds(first, 2 * count)].reshape(count, 2, 8, 128)
        clev[pl.ds(offsets[h], count)] = (c[:, 0] + c[:, 1]) * 0.5
        step = min(count, 8)
        for j in range(0, count, step):
            climb(src, first + 2 * j, ulev, offsets[h] + j, step)

    root = offsets[local]
    if top:
        snd[0, 0:32] = ulev[root]
        snd[0, 32:40] = clev[root]
        rounds[0].start()

    def scale_of(h):
        return RADIUS * GROWTH**h

    for h in range(1, local):
        scale = scale_of(h)

        def couple_pair(p, scale=scale, base=offsets[h]):
            even = base + 2 * p
            gap = clev[even] - clev[even + 1]
            ends = jnp.concatenate([as_link(gap, units, scale), as_link(-gap, units, scale)], axis=1)
            shape = scale * scale * unit_gaps[...] + DELTA_SQ
            shapes = jnp.concatenate([shape, shape], axis=1)
            to_even, to_odd = tiles(unit_left[...], target_feats(ends), shapes)
            vlev[even] = fold(dot(stacked(ulev[even + 1]), to_even))
            vlev[even + 1] = fold(dot(stacked(ulev[even]), to_odd))

        pairs = leaf_dev >> (h + 1)
        unroll = min(pairs, 4)

        def pair_step(i, _, couple_pair=couple_pair, unroll=unroll):
            for k in range(unroll):
                couple_pair(i * unroll + k)
            return 0

        lax.fori_loop(0, pairs // unroll, pair_step, 0)

    c_left.wait()
    c_right.wait()
    for side, base in ((1, 0), (2, half + leaf_dev)):
        got = cmsg[side]
        for k in range(half):
            col = k + half if side == 1 else k
            wide_c[base + k] = jnp.broadcast_to(got[:, col : col + 1], (8, 128))
    u_left.wait()
    u_right.wait()

    def ready(i, _):
        for k in range(8):
            j = i * 8 + k
            wide_w[j] = stacked(wide_u[j])
            wide_w[half + leaf_dev + j] = stacked(wide_u[half + leaf_dev + j])
        return 0

    lax.fori_loop(0, half // 8, ready, 0)

    first_leaf = me * leaf_dev - half
    shape0 = scale_of(0) * units

    def far_leaf(l):
        own = wide_c[half + l] + shape0
        total = None
        for s in range(0, far.shape[0], 2):
            i, j = ((far[t, l] - first_leaf) & (2 * leaf_dev - 1) for t in (s, s + 1))
            ends = [as_target(own - wide_c[i], scale_of(0)), as_target(own - wide_c[j], scale_of(0))]
            g = tiles(unit_left[...], target_feats(jnp.concatenate(ends, axis=1)))
            r = dot(jnp.concatenate([wide_w[i], wide_w[j]], axis=1), jnp.concatenate(g, axis=0))
            total = r if total is None else total + r
        vfar[l] = fold(total)

    def far_step(i, _):
        far_leaf(2 * i)
        far_leaf(2 * i + 1)
        return 0

    steps = half
    for b in range(top):
        lax.fori_loop(b * steps // top, (b + 1) * steps // top, far_step, 0)
        rounds[b].wait()
        if b + 1 < top:
            mine, theirs = snd[b, 0:32], rcv[b, 0:32]
            low = bits[b] == 0
            u = merge(jnp.where(low, mine, theirs), jnp.where(low, theirs, mine))
            snd[b + 1, 0:32] = u
            snd[b + 1, 32:40] = (snd[b, 32:40] + rcv[b, 32:40]) * 0.5
            rounds[b + 1].start()

    def lower(v):
        m = v.shape[0]
        r = dot_nt(stacked(v), down_mat[...])
        both = r[:m, :256] + (r[:m, 256:] + r[m:, :256])
        return both[:, :128], both[:, 128:]

    coupled = []
    for b in range(top):
        scale = scale_of(local + b)
        ends = as_link(snd[b, 32:40] - rcv[b, 32:40], units, scale)
        shape = scale * scale * unit_gaps[...] + DELTA_SQ
        (g,) = tiles(unit_left[...], target_feats(ends), shape)
        coupled.append(fold(dot(stacked(rcv[b, 0:32]), g)))
    field = jnp.zeros((32, 128), F32)
    for b in reversed(range(top)):
        lo, hi = lower(field)
        field = jnp.where(bits[b] == 0, lo, hi) + coupled[b]

    def descend(v, dst, to):
        count = v.shape[0]
        lo, hi = lower(v.reshape(count * 32, 128))
        kids = jnp.stack([lo.reshape(count, 32, 128), hi.reshape(count, 32, 128)], axis=1)
        where = pl.ds(to, 2 * count)
        dst[where] = dst[where] + kids.reshape(2 * count, 32, 128)

    descend(field.reshape(1, 32, 128), vlev, offsets[local - 1])
    for h in range(local - 2, -1, -1):
        parents = leaf_dev >> (h + 1)
        dst, to = (vfar, 0) if h == 0 else (vlev, offsets[h])
        step = min(parents, 8)
        for j in range(0, parents, step):
            descend(vlev[pl.ds(offsets[h + 1] + j, step)], dst, to + 2 * j)

    def leaf_out(i, _):
        for k in range(group):
            l = i * group + k
            span_l = pl.ds(pl.multiple_of(l * 128, 128), 128)
            out[:, span_l] = fold(dot_nt(stacked(vfar[l]), stacked(bases[l])))
        return 0

    lax.fori_loop(0, leaf_dev // group, leaf_out, 0)
    for copy in halo:
        copy.wait()


def near_kernel(
    near,
    count,
    first,
    pos,
    chg,
    pos_l,
    pos_r,
    chg_l,
    chg_r,
    far_part,
    out,
    feats,
    targets,
    weights,
    acc,
    items,
):
    leaf_dev = near.shape[1]
    half = leaf_dev // 2
    wide = 2 * leaf_dev
    unroll = 8

    def prepare(j, x, q):
        feats[j] = source_feats(as_source(x))
        weights[j] = stacked(q)

    def side_step(i, _):
        for k in range(4):
            j = i * 4 + k
            lanes = pl.ds(pl.multiple_of(j * 128, 128), 128)
            prepare(j, rows3(pos_l, lanes), chg_l[:, lanes])
            prepare(half + leaf_dev + j, rows3(pos_r, lanes), chg_r[:, lanes])
        return 0

    lax.fori_loop(0, half // 4, side_step, 0)

    def own_step(i, at):
        for k in range(4):
            l = i * 4 + k
            lanes = pl.ds(pl.multiple_of(l * 128, 128), 128)
            x = rows3(pos, lanes)
            prepare(half + l, x, chg[:, lanes])
            targets[l] = target_feats(as_target(x, 1.0))
            acc[l] = far_part[:, lanes]
            used = count[l]
            for s in range(0, near.shape[0], 2):
                items[3 * at] = l
                items[3 * at + 1] = (near[s, l] - first[0]) & (wide - 1)
                items[3 * at + 2] = jnp.where(s + 1 < used, (near[s + 1, l] - first[0]) & (wide - 1), wide)
                at = at + (s < used).astype(jnp.int32)
        return at

    total = lax.fori_loop(0, leaf_dev // 4, own_step, jnp.int32(0))
    nothing = jnp.zeros((8, 128), F32)
    prepare(wide, nothing, jnp.zeros((32, 128), F32))
    targets[leaf_dev] = target_feats(as_target(nothing, 1.0))
    acc[leaf_dev] = jnp.zeros((32, 128), F32)
    for k in range(unroll):
        items[3 * (total + k)] = leaf_dev
        items[3 * (total + k) + 1] = wide
        items[3 * (total + k) + 2] = wide

    def item_step(i, _):
        for k in range(unroll):
            at = 3 * (i * unroll + k)
            l, s, t = items[at], items[at + 1], items[at + 2]
            left = jnp.concatenate([feats[s], feats[t]], axis=0)
            (g,) = tiles(left, targets[l])
            r = dot(jnp.concatenate([weights[s], weights[t]], axis=1), g)
            acc[l] += fold(r)
        return 0

    lax.fori_loop(0, (total + unroll - 1) // unroll, item_step, 0)

    def out_step(i, _):
        for k in range(8):
            l = i * 8 + k
            out[:, pl.ds(pl.multiple_of(l * 128, 128), 128)] = acc[l]
        return 0

    lax.fori_loop(0, leaf_dev // 8, out_step, 0)


def shards(n, positions, charges, bases, transfer, unit_nodes, near_list, near_count, far_list):
    leaf_dev = bases.shape[0]
    half, wide = leaf_dev // 2, 2 * leaf_dev
    top = n.bit_length() - 1
    vmem = pl.BlockSpec(memory_space=pltpu.VMEM)
    smem = pl.BlockSpec(memory_space=pltpu.SMEM)
    hbm = pl.BlockSpec(memory_space=pltpu.HBM)
    span = half * 128
    shape = jax.ShapeDtypeStruct
    far_part, pos_l, pos_r, chg_l, chg_r = pl.pallas_call(
        functools.partial(tree_kernel, n),
        out_shape=[
            shape((32, leaf_dev * 128), F32),
            shape((3, span), F32),
            shape((3, span), F32),
            shape((32, span), F32),
            shape((32, span), F32),
        ],
        in_specs=[hbm] * 5 + [smem],
        out_specs=[vmem] * 5,
        scratch_shapes=[
            pltpu.VMEM((3, leaf_dev * 128), F32),
            pltpu.VMEM((32, leaf_dev * 128), F32),
            pltpu.VMEM((leaf_dev, 128, 128), F32),
            pltpu.VMEM((2, 128, 128), F32),
            pltpu.VMEM((3, 128), F32),
            pltpu.VMEM((wide, 32, 128), F32),
            pltpu.VMEM((wide, 64, 128), BF16),
            pltpu.VMEM((wide, 8, 128), F32),
            pltpu.VMEM((leaf_dev, 32, 128), F32),
            pltpu.VMEM((leaf_dev, 8, 128), F32),
            pltpu.VMEM((leaf_dev, 32, 128), F32),
            pltpu.VMEM((leaf_dev, 32, 128), F32),
            pltpu.VMEM((256, 256), BF16),
            pltpu.VMEM((512, 128), BF16),
            pltpu.VMEM((128, FEATS), BF16),
            pltpu.VMEM((128, 128), F32),
            pltpu.VMEM((3, 8, 128), F32),
            pltpu.VMEM((max(top, 1), 40, 128), F32),
            pltpu.VMEM((max(top, 1), 40, 128), F32),
            pltpu.SemaphoreType.DMA((8 + top,)),
            pltpu.SemaphoreType.DMA((8 + top,)),
            pltpu.SemaphoreType.DMA((4 + leaf_dev // 8,)),
        ],
        compiler_params=pltpu.CompilerParams(
            collective_id=0, has_side_effects=True, vmem_limit_bytes=56 << 20
        ),
        name="tree",
    )(positions, charges, bases, transfer, unit_nodes, far_list.T)
    first = (lax.axis_index("leaf") * leaf_dev - half).astype(jnp.int32).reshape(1)
    return pl.pallas_call(
        near_kernel,
        out_shape=shape((32, leaf_dev * 128), F32),
        in_specs=[smem] * 3 + [vmem] * 7,
        out_specs=vmem,
        scratch_shapes=[
            pltpu.VMEM((wide + 1, 128, FEATS), BF16),
            pltpu.VMEM((leaf_dev + 1, FEATS, 128), BF16),
            pltpu.VMEM((wide + 1, 64, 128), BF16),
            pltpu.VMEM((leaf_dev + 1, 32, 128), F32),
            pltpu.SMEM((3 * (4 * leaf_dev + 8),), jnp.int32),
        ],
        compiler_params=pltpu.CompilerParams(vmem_limit_bytes=56 << 20),
        name="near",
    )(near_list.T, near_count, first, positions, charges, pos_l, pos_r, chg_l, chg_r, far_part)


def solution(mesh):
    placed = (
        P(None, "leaf"),
        P(None, "leaf"),
        P("leaf", None, None),
        P(),
        P(),
        P("leaf", None),
        P("leaf"),
        P("leaf", None),
    )
    return jax.shard_map(
        functools.partial(shards, mesh.shape["leaf"]),
        mesh=mesh,
        in_specs=placed,
        out_specs=P(None, "leaf"),
        check_vma=False,
    )
```

```python
import functools

import jax
import jax.numpy as jnp
from jax import lax
from jax.experimental import pallas as pl
from jax.experimental.pallas import tpu as pltpu
from jax.sharding import PartitionSpec as P

DELTA_SQ = 0.0625
RADIUS = 0.4
GROWTH = 1.26
F32, BF16 = jnp.float32, jnp.bfloat16
MESH = pl.DeviceIdType.MESH
NT = (((1,), (1,)), ((), ()))
FEATS = 48


def dot(a, b):
    return jnp.dot(a, b, preferred_element_type=F32)


def dot_nt(a, b):
    return lax.dot_general(a, b, NT, preferred_element_type=F32)


def halves(x):
    hi = x.astype(BF16)
    return hi, (x - hi.astype(F32)).astype(BF16)


def thirds(x):
    a = x.astype(BF16).astype(F32)
    rest = x - a
    b = rest.astype(BF16).astype(F32)
    return a, b, rest - b


def stacked(x):
    hi, lo = halves(x)
    return jnp.concatenate([hi, lo], axis=0)


def target_feats(y):
    a, b, c = thirds(y)
    return jnp.concatenate([a, a, a, b, b, c], axis=0).astype(BF16)


def source_feats(x):
    a, b, c = thirds(x)
    return jnp.concatenate([a, b, c, a, b, a], axis=0).T.astype(BF16)


def row_ids():
    return lax.broadcasted_iota(jnp.int32, (8, 128), 0)


def rows3(ref, lanes):
    rows = row_ids()
    x = jnp.where(rows == 0, ref[0:1, lanes], 0.0)
    x = jnp.where(rows == 1, ref[1:2, lanes], x)
    return jnp.where(rows == 2, ref[2:3, lanes], x)


def as_source(x):
    rows = row_ids()
    norm = jnp.sum(x * x, axis=0, keepdims=True)
    return jnp.where(rows == 3, 1.0, jnp.where(rows == 4, norm, -2.0 * x))


def as_target(y, scale):
    rows = row_ids()
    norm = jnp.sum(y * y, axis=0, keepdims=True)
    return jnp.where(rows == 3, norm + DELTA_SQ, jnp.where(rows == 4, scale * scale, scale * y))


def as_link(gap, units, scale):
    rest = jnp.sum(gap * (gap + (2.0 * scale) * units), axis=0, keepdims=True)
    return jnp.where(row_ids() == 3, rest, scale * gap)


def fold(r):
    m, n = r.shape[0] // 2, r.shape[1] // 2
    return r[:m, :n] + (r[:m, n:] + r[m:, :n]) + r[m:, n:]


def tiles(left, right, extra=None):
    dist_sq = dot(left, right)
    hi, lo = halves(lax.rsqrt(dist_sq if extra is None else dist_sq + extra))
    return [
        jnp.concatenate([hi[:, i : i + 128], lo[:, i : i + 128]], axis=1)
        for i in range(0, right.shape[1], 128)
    ]


def tree_kernel(
    n,
    pos_in,
    chg_in,
    bases_in,
    transfer_in,
    unit_in,
    far,
    out,
    halo_pos_l,
    halo_pos_r,
    halo_chg_l,
    halo_chg_r,
    pos,
    chg,
    bases,
    transfer,
    unit,
    wide_u,
    wide_w,
    wide_c,
    ulev,
    clev,
    vlev,
    vfar,
    up_mat,
    down_mat,
    unit_left,
    unit_gaps,
    node_s,
    node_t,
    cmsg,
    snd,
    rcv,
    outs,
    send_sem,
    recv_sem,
    load_sem,
    store_sem,
):
    me = lax.axis_index("leaf")
    leaf_dev = bases_in.shape[0]
    half = leaf_dev // 2
    local = leaf_dev.bit_length() - 1
    top = n.bit_length() - 1
    left, right = lax.rem(me + n - 1, n), lax.rem(me + 1, n)
    bits = [(me // (1 << b)) % 2 for b in range(top)]
    partners = [me + (1 << b) * (1 - 2 * bits[b]) for b in range(top)]
    offsets = [0] * (local + 1)
    for h in range(2, local + 1):
        offsets[h] = offsets[h - 1] + (leaf_dev >> (h - 1))

    group = 8
    parts = leaf_dev // group
    order = [j for k in range(parts // 2) for j in (k, parts - 1 - k)]
    loads = [
        pltpu.make_async_copy(src, dst, load_sem.at[i])
        for i, (src, dst) in enumerate(
            [(chg_in, chg), (pos_in, pos), (transfer_in, transfer), (unit_in, unit)]
            + [(bases_in.at[pl.ds(j * group, group)], bases.at[pl.ds(j * group, group)]) for j in order]
        )
    ]
    for copy in loads[:2] + loads[4:] + loads[2:4]:
        copy.start()
    barrier = pltpu.get_barrier_semaphore()
    for other in [left, right] + partners:
        pl.semaphore_signal(barrier, inc=1, device_id=(other,), device_id_type=MESH)

    def remote(src, dst, which, device):
        return pltpu.make_async_remote_copy(
            src_ref=src,
            dst_ref=dst,
            send_sem=send_sem.at[which],
            recv_sem=recv_sem.at[which],
            device_id=(device,),
            device_id_type=MESH,
        )

    chunks = parts // 2
    u_left, u_right = [], []
    for k in range(chunks):
        src, dst = half + k * group, half + leaf_dev + k * group
        u_left.append(remote(wide_u.at[pl.ds(src, group)], wide_u.at[pl.ds(dst, group)], k, left))
        src, dst = half + leaf_dev - (k + 1) * group, half - (k + 1) * group
        u_right.append(
            remote(wide_u.at[pl.ds(src, group)], wide_u.at[pl.ds(dst, group)], chunks + k, right)
        )
    at = 2 * chunks
    c_left = remote(cmsg.at[0], cmsg.at[2], at, left)
    c_right = remote(cmsg.at[0], cmsg.at[1], at + 1, right)
    span = group * 128
    halo = [
        remote(pos_in.at[:, pl.ds(0, half * 128)], halo_pos_r, at + 2, left),
        remote(pos_in.at[:, pl.ds(half * 128, half * 128)], halo_pos_l, at + 3, right),
    ]
    for k in range(chunks):
        lanes = pl.ds(k * span, span)
        halo.append(remote(chg.at[:, lanes], halo_chg_r.at[:, lanes], at + 4 + k, left))
        mine = pl.ds(half * 128 + k * span, span)
        halo.append(remote(chg.at[:, mine], halo_chg_l.at[:, lanes], at + 4 + chunks + k, right))
    at = at + 4 + 2 * chunks
    rounds = [remote(snd.at[b], rcv.at[b], at + b, partners[b]) for b in range(top)]

    lanes_id = lax.broadcasted_iota(jnp.int32, (8, 128), 1)

    def leaf_group(i, cols):
        loads[4 + order.index(i)].wait()
        for k in range(group):
            l = i * group + k
            span_l = pl.ds(l * 128, 128)
            hi, lo = halves(bases[l])
            u = fold(dot(stacked(chg[:, span_l]), jnp.concatenate([hi, lo], axis=1)))
            wide_u[half + l] = u
            wide_w[half + l] = stacked(u)
            center = jnp.sum(rows3(pos, span_l), axis=1, keepdims=True) * (1.0 / 128)
            wide_c[half + l] = jnp.broadcast_to(center, (8, 128))
            cols = jnp.where(lanes_id == l, center, cols)
        return cols

    cols = jnp.zeros((8, 128), F32)
    for copy in loads[:2]:
        copy.wait()
    for k in range(chunks):
        cols = leaf_group(k, cols)
        cols = leaf_group(parts - 1 - k, cols)
        if k == 0:
            pl.semaphore_wait(barrier, top + 2)
        if k < 2:
            u_left[k].start()
            u_right[k].start()
    cmsg[0] = cols
    c_left.start()
    c_right.start()
    for copy in loads[2:4]:
        copy.wait()

    t0, t1 = transfer[0], transfer[1]
    h0, l0 = halves(t0)
    h1, l1 = halves(t1)
    up_mat[...] = jnp.concatenate(
        [jnp.concatenate([h0, l0], axis=1), jnp.concatenate([h1, l1], axis=1)], axis=0
    )
    down_mat[...] = jnp.concatenate([h0, h1, l0, l1], axis=0)
    units = rows3(unit, slice(None))
    unit_left[...] = source_feats(as_source(units))
    columns = units.T
    gaps = [columns[:, c : c + 1] - units[c : c + 1, :] for c in range(3)]
    unit_gaps[...] = gaps[0] * gaps[0] + gaps[1] * gaps[1] + gaps[2] * gaps[2]
    def merge(even, odd):
        m = even.shape[0]
        r = dot(stacked(jnp.concatenate([even, odd], axis=1)), up_mat[...])
        return r[:m, :128] + (r[:m, 128:] + r[m:, :128])

    def climb(src, first, dst, to, count):
        x = src[pl.ds(first, 2 * count)].reshape(count, 2, 32, 128)
        u = merge(x[:, 0].reshape(count * 32, 128), x[:, 1].reshape(count * 32, 128))
        dst[pl.ds(to, count)] = u.reshape(count, 32, 128)

    for h in range(1, local + 1):
        count = leaf_dev >> h
        src, first = (wide_u, half) if h == 1 else (ulev, offsets[h - 1])
        csrc = wide_c if h == 1 else clev
        c = csrc[pl.ds(first, 2 * count)].reshape(count, 2, 8, 128)
        clev[pl.ds(offsets[h], count)] = (c[:, 0] + c[:, 1]) * 0.5
        step = min(count, 8)
        for j in range(0, count, step):
            climb(src, first + 2 * j, ulev, offsets[h] + j, step)

    root = offsets[local]
    if top:
        snd[0, 0:32] = ulev[root]
        snd[0, 32:40] = clev[root]
        rounds[0].start()

    def scale_of(h):
        return RADIUS * GROWTH**h

    for h in range(1, local):
        scale = scale_of(h)

        def couple_pair(p, scale=scale, base=offsets[h]):
            even = base + 2 * p
            gap = clev[even] - clev[even + 1]
            ends = jnp.concatenate([as_link(gap, units, scale), as_link(-gap, units, scale)], axis=1)
            shape = scale * scale * unit_gaps[...] + DELTA_SQ
            shapes = jnp.concatenate([shape, shape], axis=1)
            to_even, to_odd = tiles(unit_left[...], target_feats(ends), shapes)
            vlev[even] = fold(dot(stacked(ulev[even + 1]), to_even))
            vlev[even + 1] = fold(dot(stacked(ulev[even]), to_odd))

        pairs = leaf_dev >> (h + 1)
        unroll = min(pairs, 4)

        def pair_step(i, _, couple_pair=couple_pair, unroll=unroll):
            for k in range(unroll):
                couple_pair(i * unroll + k)
            return 0

        lax.fori_loop(0, pairs // unroll, pair_step, 0)

    def advance(b):
        rounds[b].wait()
        if b + 1 < top:
            mine, theirs = snd[b, 0:32], rcv[b, 0:32]
            low = bits[b] == 0
            u = merge(jnp.where(low, mine, theirs), jnp.where(low, theirs, mine))
            snd[b + 1, 0:32] = u
            snd[b + 1, 32:40] = (snd[b, 32:40] + rcv[b, 32:40]) * 0.5
            rounds[b + 1].start()

    if top:
        advance(0)

    shape0 = scale_of(0) * units - clev[root]

    def own_nodes(i, _):
        for k in range(8):
            l = i * 8 + k
            x = wide_c[half + l] + shape0
            node_s[half + l] = source_feats(as_source(x))
            node_t[l] = target_feats(as_target(x, 1.0))
        return 0

    lax.fori_loop(0, leaf_dev // 8, own_nodes, 0)
    if top > 1:
        advance(1)
    c_left.wait()
    c_right.wait()
    first_leaf = me * leaf_dev - half

    def far_leaf(l):
        total = None
        for s in range(0, far.shape[0], 2):
            i, j = ((far[t, l] - first_leaf) & (2 * leaf_dev - 1) for t in (s, s + 1))
            (g,) = tiles(jnp.concatenate([node_s[i], node_s[j]], axis=0), node_t[l])
            r = dot(jnp.concatenate([wide_w[i], wide_w[j]], axis=1), g)
            total = fold(r) if total is None else total + fold(r)
        vfar[l] = total

    def lower(v):
        m = v.shape[0]
        r = dot_nt(stacked(v), down_mat[...])
        both = r[:m, :256] + (r[:m, 256:] + r[m:, :256])
        return both[:, :128], both[:, 128:]

    def descend(v, dst, to):
        count = v.shape[0]
        lo, hi = lower(v.reshape(count * 32, 128))
        kids = jnp.stack([lo.reshape(count, 32, 128), hi.reshape(count, 32, 128)], axis=1)
        where = pl.ds(to, 2 * count)
        dst[where] = dst[where] + kids.reshape(2 * count, 32, 128)

    def inner():
        coupled = []
        for b in range(top):
            scale = scale_of(local + b)
            ends = as_link(snd[b, 32:40] - rcv[b, 32:40], units, scale)
            shape = scale * scale * unit_gaps[...] + DELTA_SQ
            (g,) = tiles(unit_left[...], target_feats(ends), shape)
            coupled.append(fold(dot(stacked(rcv[b, 0:32]), g)))
        field = jnp.zeros((32, 128), F32)
        for b in reversed(range(top)):
            lo, hi = lower(field)
            field = jnp.where(bits[b] == 0, lo, hi) + coupled[b]
        descend(field.reshape(1, 32, 128), vlev, offsets[local - 1])
        for h in range(local - 2, 0, -1):
            parents = leaf_dev >> (h + 1)
            step = min(parents, 8)
            for j in range(0, parents, step):
                descend(vlev[pl.ds(offsets[h + 1] + j, step)], vlev, offsets[h] + 2 * j)

    def far_group(g):
        def step(i, _):
            for k in range(4):
                far_leaf(g * group + i * 4 + k)
            return 0

        lax.fori_loop(0, group // 4, step, 0)

    b = 2
    pieces = list(halo)
    for k in range(chunks):
        u_left[k].wait()
        u_right[k].wait()
        if k + 2 < chunks:
            u_left[k + 2].start()
            u_right[k + 2].start()
        for side in (1, 2):
            got = cmsg[side]
            for m in range(group):
                j = half - (k + 1) * group + m if side == 1 else half + leaf_dev + k * group + m
                col = leaf_dev - (k + 1) * group + m if side == 1 else k * group + m
                c = jnp.broadcast_to(got[:, col : col + 1], (8, 128))
                node_s[j] = source_feats(as_source(c + shape0))
                wide_w[j] = stacked(wide_u[j])
        for g in (chunks - 1 - k, chunks + k):
            if g == parts - 1:
                while b < top:
                    advance(b)
                    b += 1
                inner()
                for m in range(group):
                    far_leaf(g * group + m)
                continue
            far_group(g)
            if b < top:
                advance(b)
                b += 1
            if k >= chunks // 2 - 1:
                for copy in pieces[:4]:
                    copy.start()
                pieces = pieces[4:]

    for j in range(0, half, 8):
        descend(vlev[pl.ds(offsets[1] + j, 8)], vfar, 2 * j)

    stores = []
    for i in range(parts // 2):
        for k in range(2 * group):
            l = i * 2 * group + k
            outs[:, pl.ds(l * 128, 128)] = fold(dot_nt(stacked(vfar[l]), stacked(bases[l])))
        lanes = pl.ds(i * 2 * span, 2 * span)
        stores.append(pltpu.make_async_copy(outs.at[:, lanes], out.at[:, lanes], store_sem.at[i]))
        stores[-1].start()
    for copy in halo + stores:
        copy.wait()


def near_kernel(
    near,
    count,
    first,
    pos_in,
    chg_in,
    pos_l_in,
    pos_r_in,
    chg_l_in,
    chg_r_in,
    far_part,
    out,
    pos,
    chg,
    pos_l,
    pos_r,
    chg_l,
    chg_r,
    feats,
    targets,
    weights,
    acc,
    items,
    load_sem,
):
    leaf_dev = near.shape[1]
    half = leaf_dev // 2
    wide = 2 * leaf_dev
    unroll = 16

    pairs = [
        (pos_in, pos),
        (pos_l_in, pos_l),
        (pos_r_in, pos_r),
        (chg_in, chg),
        (chg_l_in, chg_l),
        (chg_r_in, chg_r),
        (far_part, out),
    ]
    loads = [pltpu.make_async_copy(s, d, load_sem.at[i]) for i, (s, d) in enumerate(pairs)]
    for copy in loads:
        copy.start()

    def prepare(j, x, q):
        feats[j] = source_feats(as_source(x))
        weights[j] = stacked(q)

    nothing = jnp.zeros((8, 128), F32)
    prepare(wide, nothing, jnp.zeros((32, 128), F32))
    targets[leaf_dev] = target_feats(as_target(nothing, 1.0))
    acc[leaf_dev] = jnp.zeros((32, 128), F32)
    for copy in loads[:6]:
        copy.wait()

    def prepare_step(i, at):
        for k in range(4):
            l = i * 4 + k
            lanes = pl.ds(pl.multiple_of(l * 128, 128), 128)
            x = rows3(pos, lanes)
            prepare(half + l, x, chg[:, lanes])
            targets[l] = target_feats(as_target(x, 1.0))
            acc[l] = jnp.zeros((32, 128), F32)
            used = count[l]
            for s in range(0, near.shape[0], 2):
                items[3 * at] = l
                items[3 * at + 1] = (near[s, l] - first[0]) & (wide - 1)
                items[3 * at + 2] = jnp.where(s + 1 < used, (near[s + 1, l] - first[0]) & (wide - 1), wide)
                at = at + (s < used).astype(jnp.int32)
        for k in range(2):
            j = i * 2 + k
            lanes = pl.ds(pl.multiple_of(j * 128, 128), 128)
            prepare(j, rows3(pos_l, lanes), chg_l[:, lanes])
            prepare(half + leaf_dev + j, rows3(pos_r, lanes), chg_r[:, lanes])
        return at

    total = lax.fori_loop(0, leaf_dev // 4, prepare_step, jnp.int32(0))
    for k in range(unroll):
        items[3 * (total + k)] = leaf_dev
        items[3 * (total + k) + 1] = wide
        items[3 * (total + k) + 2] = wide

    def item_step(i, _):
        for k in range(unroll):
            at = 3 * (i * unroll + k)
            l, s, t = items[at], items[at + 1], items[at + 2]
            left = jnp.concatenate([feats[s], feats[t]], axis=0)
            (g,) = tiles(left, targets[l])
            r = dot(jnp.concatenate([weights[s], weights[t]], axis=1), g)
            acc[l] += fold(r)
        return 0

    lax.fori_loop(0, (total + unroll - 1) // unroll, item_step, 0)
    loads[6].wait()

    def out_step(i, _):
        for k in range(8):
            l = i * 8 + k
            out[:, pl.ds(pl.multiple_of(l * 128, 128), 128)] += acc[l]
        return 0

    lax.fori_loop(0, leaf_dev // 8, out_step, 0)


def shards(n, positions, charges, bases, transfer, unit_nodes, near_list, near_count, far_list):
    leaf_dev = bases.shape[0]
    half, wide = leaf_dev // 2, 2 * leaf_dev
    top = n.bit_length() - 1
    vmem = pl.BlockSpec(memory_space=pltpu.VMEM)
    smem = pl.BlockSpec(memory_space=pltpu.SMEM)
    hbm = pl.BlockSpec(memory_space=pltpu.HBM)
    span = half * 128
    shape = jax.ShapeDtypeStruct
    far_part, pos_l, pos_r, chg_l, chg_r = pl.pallas_call(
        functools.partial(tree_kernel, n),
        out_shape=[
            shape((32, leaf_dev * 128), F32),
            shape((3, span), F32),
            shape((3, span), F32),
            shape((32, span), F32),
            shape((32, span), F32),
        ],
        in_specs=[hbm] * 5 + [smem],
        out_specs=[hbm] * 5,
        scratch_shapes=[
            pltpu.VMEM((3, leaf_dev * 128), F32),
            pltpu.VMEM((32, leaf_dev * 128), F32),
            pltpu.VMEM((leaf_dev, 128, 128), F32),
            pltpu.VMEM((2, 128, 128), F32),
            pltpu.VMEM((3, 128), F32),
            pltpu.VMEM((wide, 32, 128), F32),
            pltpu.VMEM((wide, 64, 128), BF16),
            pltpu.VMEM((wide, 8, 128), F32),
            pltpu.VMEM((leaf_dev, 32, 128), F32),
            pltpu.VMEM((leaf_dev, 8, 128), F32),
            pltpu.VMEM((leaf_dev, 32, 128), F32),
            pltpu.VMEM((leaf_dev, 32, 128), F32),
            pltpu.VMEM((256, 256), BF16),
            pltpu.VMEM((512, 128), BF16),
            pltpu.VMEM((128, FEATS), BF16),
            pltpu.VMEM((128, 128), F32),
            pltpu.VMEM((wide, 128, FEATS), BF16),
            pltpu.VMEM((leaf_dev, FEATS, 128), BF16),
            pltpu.VMEM((3, 8, 128), F32),
            pltpu.VMEM((max(top, 1), 40, 128), F32),
            pltpu.VMEM((max(top, 1), 40, 128), F32),
            pltpu.VMEM((32, leaf_dev * 128), F32),
            pltpu.SemaphoreType.DMA((leaf_dev // 4 + 4 + top,)),
            pltpu.SemaphoreType.DMA((leaf_dev // 4 + 4 + top,)),
            pltpu.SemaphoreType.DMA((4 + leaf_dev // 8,)),
            pltpu.SemaphoreType.DMA((leaf_dev // 16,)),
        ],
        compiler_params=pltpu.CompilerParams(
            collective_id=0, has_side_effects=True, vmem_limit_bytes=56 << 20
        ),
        name="tree",
    )(positions, charges, bases, transfer, unit_nodes, far_list.T)
    first = (lax.axis_index("leaf") * leaf_dev - half).astype(jnp.int32).reshape(1)
    return pl.pallas_call(
        near_kernel,
        out_shape=shape((32, leaf_dev * 128), F32),
        in_specs=[smem] * 3 + [hbm] * 7,
        out_specs=vmem,
        scratch_shapes=[
            pltpu.VMEM((3, leaf_dev * 128), F32),
            pltpu.VMEM((32, leaf_dev * 128), F32),
            pltpu.VMEM((3, span), F32),
            pltpu.VMEM((3, span), F32),
            pltpu.VMEM((32, span), F32),
            pltpu.VMEM((32, span), F32),
            pltpu.VMEM((wide + 1, 128, FEATS), BF16),
            pltpu.VMEM((leaf_dev + 1, FEATS, 128), BF16),
            pltpu.VMEM((wide + 1, 64, 128), BF16),
            pltpu.VMEM((leaf_dev + 1, 32, 128), F32),
            pltpu.SMEM((3 * (4 * leaf_dev + 16),), jnp.int32),
            pltpu.SemaphoreType.DMA((7,)),
        ],
        compiler_params=pltpu.CompilerParams(vmem_limit_bytes=56 << 20),
        name="near",
    )(near_list.T, near_count, first, positions, charges, pos_l, pos_r, chg_l, chg_r, far_part)


def solution(mesh):
    placed = (
        P(None, "leaf"),
        P(None, "leaf"),
        P("leaf", None, None),
        P(),
        P(),
        P("leaf", None),
        P("leaf"),
        P("leaf", None),
    )
    return jax.shard_map(
        functools.partial(shards, mesh.shape["leaf"]),
        mesh=mesh,
        in_specs=placed,
        out_specs=P(None, "leaf"),
        check_vma=False,
    )
```

```python
import functools

import jax
import jax.numpy as jnp
from jax import lax
from jax.experimental import pallas as pl
from jax.experimental.pallas import tpu as pltpu
from jax.sharding import PartitionSpec as P

DELTA_SQ = 0.0625
RADIUS = 0.4
GROWTH = 1.26
F32, BF16 = jnp.float32, jnp.bfloat16
MESH = pl.DeviceIdType.MESH
NT = (((1,), (1,)), ((), ()))
FEATS = 48


def dot(a, b):
    return jnp.dot(a, b, preferred_element_type=F32)


def dot_nt(a, b):
    return lax.dot_general(a, b, NT, preferred_element_type=F32)


def halves(x):
    hi = x.astype(BF16)
    return hi, (x - hi.astype(F32)).astype(BF16)


def thirds(x):
    a = x.astype(BF16).astype(F32)
    rest = x - a
    b = rest.astype(BF16).astype(F32)
    return a, b, rest - b


def stacked(x):
    hi, lo = halves(x)
    return jnp.concatenate([hi, lo], axis=0)


def target_feats(y):
    a, b, c = thirds(y)
    return jnp.concatenate([a, a, a, b, b, c], axis=0).astype(BF16)


def source_feats(x):
    a, b, c = thirds(x)
    return jnp.concatenate([a, b, c, a, b, a], axis=0).T.astype(BF16)


def row_ids():
    return lax.broadcasted_iota(jnp.int32, (8, 128), 0)


def rows3(ref, lanes):
    rows = row_ids()
    x = jnp.where(rows == 0, ref[0:1, lanes], 0.0)
    x = jnp.where(rows == 1, ref[1:2, lanes], x)
    return jnp.where(rows == 2, ref[2:3, lanes], x)


def as_source(x):
    rows = row_ids()
    norm = jnp.sum(x * x, axis=0, keepdims=True)
    return jnp.where(rows == 3, 1.0, jnp.where(rows == 4, norm, -2.0 * x))


def as_target(y, scale):
    rows = row_ids()
    norm = jnp.sum(y * y, axis=0, keepdims=True)
    return jnp.where(rows == 3, norm + DELTA_SQ, jnp.where(rows == 4, scale * scale, scale * y))


def as_link(gap, units, scale):
    rest = jnp.sum(gap * (gap + (2.0 * scale) * units), axis=0, keepdims=True)
    return jnp.where(row_ids() == 3, rest, scale * gap)


def fold(r):
    m, n = r.shape[0] // 2, r.shape[1] // 2
    return r[:m, :n] + (r[:m, n:] + r[m:, :n]) + r[m:, n:]


def tiles(left, right, extra=None):
    dist_sq = dot(left, right)
    hi, lo = halves(lax.rsqrt(dist_sq if extra is None else dist_sq + extra))
    return [
        jnp.concatenate([hi[:, i : i + 128], lo[:, i : i + 128]], axis=1)
        for i in range(0, right.shape[1], 128)
    ]


def tree_kernel(
    n,
    pos_in,
    chg_in,
    bases_in,
    transfer_in,
    unit_in,
    far,
    out,
    halo_pos_l,
    halo_pos_r,
    halo_chg_l,
    halo_chg_r,
    pos,
    chg,
    bases,
    transfer,
    unit,
    wide_u,
    wide_w,
    wide_c,
    ulev,
    clev,
    vlev,
    vfar,
    up_mat,
    down_mat,
    unit_left,
    unit_gaps,
    node_s,
    node_t,
    cmsg,
    snd,
    rcv,
    outs,
    send_sem,
    recv_sem,
    load_sem,
    store_sem,
):
    me = lax.axis_index("leaf")
    leaf_dev = bases_in.shape[0]
    half = leaf_dev // 2
    local = leaf_dev.bit_length() - 1
    top = n.bit_length() - 1
    left, right = lax.rem(me + n - 1, n), lax.rem(me + 1, n)
    bits = [(me // (1 << b)) % 2 for b in range(top)]
    partners = [me + (1 << b) * (1 - 2 * bits[b]) for b in range(top)]
    offsets = [0] * (local + 1)
    for h in range(2, local + 1):
        offsets[h] = offsets[h - 1] + (leaf_dev >> (h - 1))

    group = 8
    parts = leaf_dev // group
    order = [j for k in range(parts // 2) for j in (k, parts - 1 - k)]
    loads = [
        pltpu.make_async_copy(src, dst, load_sem.at[i])
        for i, (src, dst) in enumerate(
            [(chg_in, chg), (pos_in, pos), (transfer_in, transfer), (unit_in, unit)]
            + [(bases_in.at[pl.ds(j * group, group)], bases.at[pl.ds(j * group, group)]) for j in order]
        )
    ]
    for copy in loads[:2] + loads[4:] + loads[2:4]:
        copy.start()
    barrier = pltpu.get_barrier_semaphore()
    for other in [left, right] + partners:
        pl.semaphore_signal(barrier, inc=1, device_id=(other,), device_id_type=MESH)

    def remote(src, dst, which, device):
        return pltpu.make_async_remote_copy(
            src_ref=src,
            dst_ref=dst,
            send_sem=send_sem.at[which],
            recv_sem=recv_sem.at[which],
            device_id=(device,),
            device_id_type=MESH,
        )

    chunks = parts // 2
    u_left, u_right = [], []
    for k in range(chunks):
        src, dst = half + k * group, half + leaf_dev + k * group
        u_left.append(remote(wide_u.at[pl.ds(src, group)], wide_u.at[pl.ds(dst, group)], k, left))
        src, dst = half + leaf_dev - (k + 1) * group, half - (k + 1) * group
        u_right.append(
            remote(wide_u.at[pl.ds(src, group)], wide_u.at[pl.ds(dst, group)], chunks + k, right)
        )
    at = 2 * chunks
    c_left = remote(cmsg.at[0], cmsg.at[2], at, left)
    c_right = remote(cmsg.at[0], cmsg.at[1], at + 1, right)
    span = group * 128
    halo = [
        remote(pos_in.at[:, pl.ds(0, half * 128)], halo_pos_r, at + 2, left),
        remote(pos_in.at[:, pl.ds(half * 128, half * 128)], halo_pos_l, at + 3, right),
    ]
    for k in range(chunks):
        lanes = pl.ds(k * span, span)
        halo.append(remote(chg.at[:, lanes], halo_chg_r.at[:, lanes], at + 4 + k, left))
        mine = pl.ds(half * 128 + k * span, span)
        halo.append(remote(chg.at[:, mine], halo_chg_l.at[:, lanes], at + 4 + chunks + k, right))
    at = at + 4 + 2 * chunks
    rounds = [remote(snd.at[b], rcv.at[b], at + b, partners[b]) for b in range(top)]

    lanes_id = lax.broadcasted_iota(jnp.int32, (8, 128), 1)

    def leaf_group(i, cols):
        loads[4 + order.index(i)].wait()
        for k in range(group):
            l = i * group + k
            span_l = pl.ds(l * 128, 128)
            hi, lo = halves(bases[l])
            u = fold(dot(stacked(chg[:, span_l]), jnp.concatenate([hi, lo], axis=1)))
            wide_u[half + l] = u
            wide_w[half + l] = stacked(u)
            center = jnp.sum(rows3(pos, span_l), axis=1, keepdims=True) * (1.0 / 128)
            wide_c[half + l] = jnp.broadcast_to(center, (8, 128))
            cols = jnp.where(lanes_id == l, center, cols)
        return cols

    cols = jnp.zeros((8, 128), F32)
    for copy in loads[:2]:
        copy.wait()
    for k in range(chunks):
        cols = leaf_group(k, cols)
        cols = leaf_group(parts - 1 - k, cols)
    cmsg[0] = cols
    for copy in loads[2:4]:
        copy.wait()

    t0, t1 = transfer[0], transfer[1]
    h0, l0 = halves(t0)
    h1, l1 = halves(t1)
    up_mat[...] = jnp.concatenate(
        [jnp.concatenate([h0, l0], axis=1), jnp.concatenate([h1, l1], axis=1)], axis=0
    )
    down_mat[...] = jnp.concatenate([h0, h1, l0, l1], axis=0)
    units = rows3(unit, slice(None))
    unit_left[...] = source_feats(as_source(units))
    columns = units.T
    gaps = [columns[:, c : c + 1] - units[c : c + 1, :] for c in range(3)]
    unit_gaps[...] = gaps[0] * gaps[0] + gaps[1] * gaps[1] + gaps[2] * gaps[2]
    def merge(even, odd):
        m = even.shape[0]
        r = dot(stacked(jnp.concatenate([even, odd], axis=1)), up_mat[...])
        return r[:m, :128] + (r[:m, 128:] + r[m:, :128])

    def climb(src, first, dst, to, count):
        x = src[pl.ds(first, 2 * count)].reshape(count, 2, 32, 128)
        u = merge(x[:, 0].reshape(count * 32, 128), x[:, 1].reshape(count * 32, 128))
        dst[pl.ds(to, count)] = u.reshape(count, 32, 128)

    for h in range(1, local + 1):
        count = leaf_dev >> h
        src, first = (wide_u, half) if h == 1 else (ulev, offsets[h - 1])
        csrc = wide_c if h == 1 else clev
        c = csrc[pl.ds(first, 2 * count)].reshape(count, 2, 8, 128)
        clev[pl.ds(offsets[h], count)] = (c[:, 0] + c[:, 1]) * 0.5
        step = min(count, 8)
        for j in range(0, count, step):
            climb(src, first + 2 * j, ulev, offsets[h] + j, step)

    root = offsets[local]
    snd[0, 0:32] = ulev[root]
    snd[0, 32:40] = clev[root]

    def scale_of(h):
        return RADIUS * GROWTH**h

    shape0 = scale_of(0) * units - clev[root]

    def own_nodes(i, _):
        for k in range(8):
            l = i * 8 + k
            x = wide_c[half + l] + shape0
            node_s[half + l] = source_feats(as_source(x))
            node_t[l] = target_feats(as_target(x, 1.0))
        return 0

    lax.fori_loop(0, leaf_dev // 8, own_nodes, 0)
    pl.semaphore_wait(barrier, top + 2)
    if top:
        rounds[0].start()
    c_left.start()
    c_right.start()
    for k in range(2):
        u_left[k].start()
        u_right[k].start()

    for h in range(1, local):
        scale = scale_of(h)

        def couple_pair(p, scale=scale, base=offsets[h]):
            even = base + 2 * p
            gap = clev[even] - clev[even + 1]
            ends = jnp.concatenate([as_link(gap, units, scale), as_link(-gap, units, scale)], axis=1)
            shape = scale * scale * unit_gaps[...] + DELTA_SQ
            shapes = jnp.concatenate([shape, shape], axis=1)
            to_even, to_odd = tiles(unit_left[...], target_feats(ends), shapes)
            vlev[even] = fold(dot(stacked(ulev[even + 1]), to_even))
            vlev[even + 1] = fold(dot(stacked(ulev[even]), to_odd))

        pairs = leaf_dev >> (h + 1)
        unroll = min(pairs, 4)

        def pair_step(i, _, couple_pair=couple_pair, unroll=unroll):
            for k in range(unroll):
                couple_pair(i * unroll + k)
            return 0

        lax.fori_loop(0, pairs // unroll, pair_step, 0)

    def advance(b):
        rounds[b].wait()
        if b + 1 < top:
            mine, theirs = snd[b, 0:32], rcv[b, 0:32]
            low = bits[b] == 0
            u = merge(jnp.where(low, mine, theirs), jnp.where(low, theirs, mine))
            snd[b + 1, 0:32] = u
            snd[b + 1, 32:40] = (snd[b, 32:40] + rcv[b, 32:40]) * 0.5
            rounds[b + 1].start()

    if top:
        advance(0)

    if top > 1:
        advance(1)
    c_left.wait()
    c_right.wait()
    first_leaf = me * leaf_dev - half

    def far_leaf(l):
        total = None
        for s in range(0, far.shape[0], 2):
            i, j = ((far[t, l] - first_leaf) & (2 * leaf_dev - 1) for t in (s, s + 1))
            (g,) = tiles(jnp.concatenate([node_s[i], node_s[j]], axis=0), node_t[l])
            r = dot(jnp.concatenate([wide_w[i], wide_w[j]], axis=1), g)
            total = fold(r) if total is None else total + fold(r)
        vfar[l] = total

    def lower(v):
        m = v.shape[0]
        r = dot_nt(stacked(v), down_mat[...])
        both = r[:m, :256] + (r[:m, 256:] + r[m:, :256])
        return both[:, :128], both[:, 128:]

    def descend(v, dst, to):
        count = v.shape[0]
        lo, hi = lower(v.reshape(count * 32, 128))
        kids = jnp.stack([lo.reshape(count, 32, 128), hi.reshape(count, 32, 128)], axis=1)
        where = pl.ds(to, 2 * count)
        dst[where] = dst[where] + kids.reshape(2 * count, 32, 128)

    def inner():
        coupled = []
        for b in range(top):
            scale = scale_of(local + b)
            ends = as_link(snd[b, 32:40] - rcv[b, 32:40], units, scale)
            shape = scale * scale * unit_gaps[...] + DELTA_SQ
            (g,) = tiles(unit_left[...], target_feats(ends), shape)
            coupled.append(fold(dot(stacked(rcv[b, 0:32]), g)))
        field = jnp.zeros((32, 128), F32)
        for b in reversed(range(top)):
            lo, hi = lower(field)
            field = jnp.where(bits[b] == 0, lo, hi) + coupled[b]
        descend(field.reshape(1, 32, 128), vlev, offsets[local - 1])
        for h in range(local - 2, 0, -1):
            parents = leaf_dev >> (h + 1)
            step = min(parents, 8)
            for j in range(0, parents, step):
                descend(vlev[pl.ds(offsets[h + 1] + j, step)], vlev, offsets[h] + 2 * j)

    def far_group(g):
        def step(i, _):
            for k in range(4):
                far_leaf(g * group + i * 4 + k)
            return 0

        lax.fori_loop(0, group // 4, step, 0)

    b = 2
    pieces = list(halo)
    for k in range(chunks):
        u_left[k].wait()
        u_right[k].wait()
        if k + 2 < chunks:
            u_left[k + 2].start()
            u_right[k + 2].start()
        for side in (1, 2):
            got = cmsg[side]
            for m in range(group):
                j = half - (k + 1) * group + m if side == 1 else half + leaf_dev + k * group + m
                col = leaf_dev - (k + 1) * group + m if side == 1 else k * group + m
                c = jnp.broadcast_to(got[:, col : col + 1], (8, 128))
                node_s[j] = source_feats(as_source(c + shape0))
                wide_w[j] = stacked(wide_u[j])
        for g in (chunks - 1 - k, chunks + k):
            if g == parts - 1:
                while b < top:
                    advance(b)
                    b += 1
                inner()
                for m in range(group):
                    far_leaf(g * group + m)
                continue
            far_group(g)
            if b < top:
                advance(b)
                b += 1
            if k >= chunks // 2 - 1:
                for copy in pieces[:4]:
                    copy.start()
                pieces = pieces[4:]

    for j in range(0, half, 8):
        descend(vlev[pl.ds(offsets[1] + j, 8)], vfar, 2 * j)

    stores = []
    for i in range(parts // 2):
        for k in range(2 * group):
            l = i * 2 * group + k
            outs[:, pl.ds(l * 128, 128)] = fold(dot_nt(stacked(vfar[l]), stacked(bases[l])))
        lanes = pl.ds(i * 2 * span, 2 * span)
        stores.append(pltpu.make_async_copy(outs.at[:, lanes], out.at[:, lanes], store_sem.at[i]))
        stores[-1].start()
    for copy in halo + stores:
        copy.wait()


def near_kernel(
    near,
    count,
    first,
    pos_in,
    chg_in,
    pos_l_in,
    pos_r_in,
    chg_l_in,
    chg_r_in,
    far_part,
    out,
    pos,
    chg,
    pos_l,
    pos_r,
    chg_l,
    chg_r,
    feats,
    targets,
    weights,
    acc,
    items,
    load_sem,
):
    leaf_dev = near.shape[1]
    half = leaf_dev // 2
    wide = 2 * leaf_dev
    unroll = 16

    pairs = [
        (pos_in, pos),
        (pos_l_in, pos_l),
        (pos_r_in, pos_r),
        (chg_in, chg),
        (chg_l_in, chg_l),
        (chg_r_in, chg_r),
        (far_part, out),
    ]
    loads = [pltpu.make_async_copy(s, d, load_sem.at[i]) for i, (s, d) in enumerate(pairs)]
    for copy in loads:
        copy.start()

    def prepare(j, x, q):
        feats[j] = source_feats(as_source(x))
        weights[j] = stacked(q)

    nothing = jnp.zeros((8, 128), F32)
    prepare(wide, nothing, jnp.zeros((32, 128), F32))
    targets[leaf_dev] = target_feats(as_target(nothing, 1.0))
    acc[leaf_dev] = jnp.zeros((32, 128), F32)
    for copy in loads[:6]:
        copy.wait()

    def prepare_step(i, at):
        for k in range(4):
            l = i * 4 + k
            lanes = pl.ds(pl.multiple_of(l * 128, 128), 128)
            x = rows3(pos, lanes)
            prepare(half + l, x, chg[:, lanes])
            targets[l] = target_feats(as_target(x, 1.0))
            acc[l] = jnp.zeros((32, 128), F32)
            used = count[l]
            for s in range(0, near.shape[0], 2):
                items[3 * at] = l
                items[3 * at + 1] = (near[s, l] - first[0]) & (wide - 1)
                items[3 * at + 2] = jnp.where(s + 1 < used, (near[s + 1, l] - first[0]) & (wide - 1), wide)
                at = at + (s < used).astype(jnp.int32)
        for k in range(2):
            j = i * 2 + k
            lanes = pl.ds(pl.multiple_of(j * 128, 128), 128)
            prepare(j, rows3(pos_l, lanes), chg_l[:, lanes])
            prepare(half + leaf_dev + j, rows3(pos_r, lanes), chg_r[:, lanes])
        return at

    total = lax.fori_loop(0, leaf_dev // 4, prepare_step, jnp.int32(0))
    for k in range(unroll):
        items[3 * (total + k)] = leaf_dev
        items[3 * (total + k) + 1] = wide
        items[3 * (total + k) + 2] = wide

    def item_step(i, _):
        for k in range(unroll):
            at = 3 * (i * unroll + k)
            l, s, t = items[at], items[at + 1], items[at + 2]
            left = jnp.concatenate([feats[s], feats[t]], axis=0)
            (g,) = tiles(left, targets[l])
            r = dot(jnp.concatenate([weights[s], weights[t]], axis=1), g)
            acc[l] += fold(r)
        return 0

    lax.fori_loop(0, (total + unroll - 1) // unroll, item_step, 0)
    loads[6].wait()

    def out_step(i, _):
        for k in range(8):
            l = i * 8 + k
            out[:, pl.ds(pl.multiple_of(l * 128, 128), 128)] += acc[l]
        return 0

    lax.fori_loop(0, leaf_dev // 8, out_step, 0)


def shards(n, positions, charges, bases, transfer, unit_nodes, near_list, near_count, far_list):
    leaf_dev = bases.shape[0]
    half, wide = leaf_dev // 2, 2 * leaf_dev
    top = n.bit_length() - 1
    vmem = pl.BlockSpec(memory_space=pltpu.VMEM)
    smem = pl.BlockSpec(memory_space=pltpu.SMEM)
    hbm = pl.BlockSpec(memory_space=pltpu.HBM)
    span = half * 128
    shape = jax.ShapeDtypeStruct
    far_part, pos_l, pos_r, chg_l, chg_r = pl.pallas_call(
        functools.partial(tree_kernel, n),
        out_shape=[
            shape((32, leaf_dev * 128), F32),
            shape((3, span), F32),
            shape((3, span), F32),
            shape((32, span), F32),
            shape((32, span), F32),
        ],
        in_specs=[hbm] * 5 + [smem],
        out_specs=[hbm] * 5,
        scratch_shapes=[
            pltpu.VMEM((3, leaf_dev * 128), F32),
            pltpu.VMEM((32, leaf_dev * 128), F32),
            pltpu.VMEM((leaf_dev, 128, 128), F32),
            pltpu.VMEM((2, 128, 128), F32),
            pltpu.VMEM((3, 128), F32),
            pltpu.VMEM((wide, 32, 128), F32),
            pltpu.VMEM((wide, 64, 128), BF16),
            pltpu.VMEM((wide, 8, 128), F32),
            pltpu.VMEM((leaf_dev, 32, 128), F32),
            pltpu.VMEM((leaf_dev, 8, 128), F32),
            pltpu.VMEM((leaf_dev, 32, 128), F32),
            pltpu.VMEM((leaf_dev, 32, 128), F32),
            pltpu.VMEM((256, 256), BF16),
            pltpu.VMEM((512, 128), BF16),
            pltpu.VMEM((128, FEATS), BF16),
            pltpu.VMEM((128, 128), F32),
            pltpu.VMEM((wide, 128, FEATS), BF16),
            pltpu.VMEM((leaf_dev, FEATS, 128), BF16),
            pltpu.VMEM((3, 8, 128), F32),
            pltpu.VMEM((max(top, 1), 40, 128), F32),
            pltpu.VMEM((max(top, 1), 40, 128), F32),
            pltpu.VMEM((32, leaf_dev * 128), F32),
            pltpu.SemaphoreType.DMA((leaf_dev // 4 + 4 + top,)),
            pltpu.SemaphoreType.DMA((leaf_dev // 4 + 4 + top,)),
            pltpu.SemaphoreType.DMA((4 + leaf_dev // 8,)),
            pltpu.SemaphoreType.DMA((leaf_dev // 16,)),
        ],
        compiler_params=pltpu.CompilerParams(
            collective_id=0, has_side_effects=True, vmem_limit_bytes=56 << 20
        ),
        name="tree",
    )(positions, charges, bases, transfer, unit_nodes, far_list.T)
    first = (lax.axis_index("leaf") * leaf_dev - half).astype(jnp.int32).reshape(1)
    return pl.pallas_call(
        near_kernel,
        out_shape=shape((32, leaf_dev * 128), F32),
        in_specs=[smem] * 3 + [hbm] * 7,
        out_specs=vmem,
        scratch_shapes=[
            pltpu.VMEM((3, leaf_dev * 128), F32),
            pltpu.VMEM((32, leaf_dev * 128), F32),
            pltpu.VMEM((3, span), F32),
            pltpu.VMEM((3, span), F32),
            pltpu.VMEM((32, span), F32),
            pltpu.VMEM((32, span), F32),
            pltpu.VMEM((wide + 1, 128, FEATS), BF16),
            pltpu.VMEM((leaf_dev + 1, FEATS, 128), BF16),
            pltpu.VMEM((wide + 1, 64, 128), BF16),
            pltpu.VMEM((leaf_dev + 1, 32, 128), F32),
            pltpu.SMEM((3 * (4 * leaf_dev + 16),), jnp.int32),
            pltpu.SemaphoreType.DMA((7,)),
        ],
        compiler_params=pltpu.CompilerParams(vmem_limit_bytes=56 << 20),
        name="near",
    )(near_list.T, near_count, first, positions, charges, pos_l, pos_r, chg_l, chg_r, far_part)


def solution(mesh):
    placed = (
        P(None, "leaf"),
        P(None, "leaf"),
        P("leaf", None, None),
        P(),
        P(),
        P("leaf", None),
        P("leaf"),
        P("leaf", None),
    )
    return jax.shard_map(
        functools.partial(shards, mesh.shape["leaf"]),
        mesh=mesh,
        in_specs=placed,
        out_specs=P(None, "leaf"),
        check_vma=False,
    )
```

```python
import functools

import jax
import jax.numpy as jnp
from jax import lax
from jax.experimental import pallas as pl
from jax.experimental.pallas import tpu as pltpu
from jax.sharding import PartitionSpec as P

DELTA_SQ = 0.0625
RADIUS = 0.4
GROWTH = 1.26
F32, BF16 = jnp.float32, jnp.bfloat16
MESH = pl.DeviceIdType.MESH
NT = (((1,), (1,)), ((), ()))
FEATS = 48


def dot(a, b):
    return jnp.dot(a, b, preferred_element_type=F32)


def dot_nt(a, b):
    return lax.dot_general(a, b, NT, preferred_element_type=F32)


def halves(x):
    hi = x.astype(BF16)
    return hi, (x - hi.astype(F32)).astype(BF16)


def thirds(x):
    a = x.astype(BF16).astype(F32)
    rest = x - a
    b = rest.astype(BF16).astype(F32)
    return a, b, rest - b


def stacked(x):
    hi, lo = halves(x)
    return jnp.concatenate([hi, lo], axis=0)


def target_feats(y):
    a, b, c = thirds(y)
    return jnp.concatenate([a, a, a, b, b, c], axis=0).astype(BF16)


def source_feats(x):
    a, b, c = thirds(x)
    return jnp.concatenate([a, b, c, a, b, a], axis=0).T.astype(BF16)


def row_ids():
    return lax.broadcasted_iota(jnp.int32, (8, 128), 0)


def rows3(ref, lanes):
    rows = row_ids()
    x = jnp.where(rows == 0, ref[0:1, lanes], 0.0)
    x = jnp.where(rows == 1, ref[1:2, lanes], x)
    return jnp.where(rows == 2, ref[2:3, lanes], x)


def as_source(x):
    rows = row_ids()
    norm = jnp.sum(x * x, axis=0, keepdims=True)
    return jnp.where(rows == 3, 1.0, jnp.where(rows == 4, norm, -2.0 * x))


def as_target(y, scale):
    rows = row_ids()
    norm = jnp.sum(y * y, axis=0, keepdims=True)
    return jnp.where(rows == 3, norm + DELTA_SQ, jnp.where(rows == 4, scale * scale, scale * y))


def as_link(gap, units, scale):
    rest = jnp.sum(gap * (gap + (2.0 * scale) * units), axis=0, keepdims=True)
    return jnp.where(row_ids() == 3, rest, scale * gap)


def fold(r):
    m, n = r.shape[0] // 2, r.shape[1] // 2
    return r[:m, :n] + (r[:m, n:] + r[m:, :n]) + r[m:, n:]


def tiles(left, right, extra=None):
    dist_sq = dot(left, right)
    hi, lo = halves(lax.rsqrt(dist_sq if extra is None else dist_sq + extra))
    return [
        jnp.concatenate([hi[:, i : i + 128], lo[:, i : i + 128]], axis=1)
        for i in range(0, right.shape[1], 128)
    ]


def tree_kernel(
    n,
    pos_in,
    chg_in,
    bases_in,
    transfer_in,
    unit_in,
    far,
    near,
    used_slots,
    out,
    halo_pos_l,
    halo_pos_r,
    halo_chg_l,
    halo_chg_r,
    near_s,
    near_t,
    near_w,
    pos,
    chg,
    bases,
    transfer,
    unit,
    wide_u,
    wide_w,
    wide_c,
    ulev,
    clev,
    vlev,
    vfar,
    up_mat,
    down_mat,
    unit_left,
    unit_gaps,
    node_s,
    node_t,
    cmsg,
    snd,
    rcv,
    outs,
    send_sem,
    recv_sem,
    load_sem,
    store_sem,
):
    me = lax.axis_index("leaf")
    leaf_dev = bases_in.shape[0]
    half = leaf_dev // 2
    local = leaf_dev.bit_length() - 1
    top = n.bit_length() - 1
    left, right = lax.rem(me + n - 1, n), lax.rem(me + 1, n)
    bits = [(me // (1 << b)) % 2 for b in range(top)]
    partners = [me + (1 << b) * (1 - 2 * bits[b]) for b in range(top)]
    offsets = [0] * (local + 1)
    for h in range(2, local + 1):
        offsets[h] = offsets[h - 1] + (leaf_dev >> (h - 1))

    group = 8
    parts = leaf_dev // group
    order = [j for k in range(parts // 2) for j in (k, parts - 1 - k)]
    loads = [
        pltpu.make_async_copy(src, dst, load_sem.at[i])
        for i, (src, dst) in enumerate(
            [(chg_in, chg), (pos_in, pos), (transfer_in, transfer), (unit_in, unit)]
            + [(bases_in.at[pl.ds(j * group, group)], bases.at[pl.ds(j * group, group)]) for j in order]
        )
    ]
    for copy in loads[:2] + loads[4:] + loads[2:4]:
        copy.start()
    barrier = pltpu.get_barrier_semaphore()
    for other in [left, right] + partners:
        pl.semaphore_signal(barrier, inc=1, device_id=(other,), device_id_type=MESH)

    def remote(src, dst, which, device):
        return pltpu.make_async_remote_copy(
            src_ref=src,
            dst_ref=dst,
            send_sem=send_sem.at[which],
            recv_sem=recv_sem.at[which],
            device_id=(device,),
            device_id_type=MESH,
        )

    chunks = parts // 2
    u_left, u_right = [], []
    for k in range(chunks):
        src, dst = half + k * group, half + leaf_dev + k * group
        u_left.append(remote(wide_u.at[pl.ds(src, group)], wide_u.at[pl.ds(dst, group)], k, left))
        src, dst = half + leaf_dev - (k + 1) * group, half - (k + 1) * group
        u_right.append(
            remote(wide_u.at[pl.ds(src, group)], wide_u.at[pl.ds(dst, group)], chunks + k, right)
        )
    at = 2 * chunks
    c_left = remote(cmsg.at[0], cmsg.at[2], at, left)
    c_right = remote(cmsg.at[0], cmsg.at[1], at + 1, right)
    span = group * 128
    halo = [
        remote(pos_in.at[:, pl.ds(0, half * 128)], halo_pos_r, at + 2, left),
        remote(pos_in.at[:, pl.ds(half * 128, half * 128)], halo_pos_l, at + 3, right),
    ]
    for k in range(chunks):
        lanes = pl.ds(k * span, span)
        halo.append(remote(chg.at[:, lanes], halo_chg_r.at[:, lanes], at + 4 + k, left))
        mine = pl.ds(half * 128 + k * span, span)
        halo.append(remote(chg.at[:, mine], halo_chg_l.at[:, lanes], at + 4 + chunks + k, right))
    at = at + 4 + 2 * chunks
    rounds = [remote(snd.at[b], rcv.at[b], at + b, partners[b]) for b in range(top)]

    lanes_id = lax.broadcasted_iota(jnp.int32, (8, 128), 1)

    def leaf_group(i, cols):
        loads[4 + order.index(i)].wait()
        for k in range(group):
            l = i * group + k
            span_l = pl.ds(l * 128, 128)
            hi, lo = halves(bases[l])
            u = fold(dot(stacked(chg[:, span_l]), jnp.concatenate([hi, lo], axis=1)))
            wide_u[half + l] = u
            wide_w[half + l] = stacked(u)
            center = jnp.sum(rows3(pos, span_l), axis=1, keepdims=True) * (1.0 / 128)
            wide_c[half + l] = jnp.broadcast_to(center, (8, 128))
            cols = jnp.where(lanes_id == l, center, cols)
        return cols

    cols = jnp.zeros((8, 128), F32)
    for copy in loads[:2]:
        copy.wait()
    for k in range(chunks):
        cols = leaf_group(k, cols)
        cols = leaf_group(parts - 1 - k, cols)
        if k == 0:
            pl.semaphore_wait(barrier, top + 2)
        if k < 2:
            u_left[k].start()
            u_right[k].start()
    cmsg[0] = cols
    c_left.start()
    c_right.start()
    for copy in loads[2:4]:
        copy.wait()

    t0, t1 = transfer[0], transfer[1]
    h0, l0 = halves(t0)
    h1, l1 = halves(t1)
    up_mat[...] = jnp.concatenate(
        [jnp.concatenate([h0, l0], axis=1), jnp.concatenate([h1, l1], axis=1)], axis=0
    )
    down_mat[...] = jnp.concatenate([h0, h1, l0, l1], axis=0)
    units = rows3(unit, slice(None))
    unit_left[...] = source_feats(as_source(units))
    columns = units.T
    gaps = [columns[:, c : c + 1] - units[c : c + 1, :] for c in range(3)]
    unit_gaps[...] = gaps[0] * gaps[0] + gaps[1] * gaps[1] + gaps[2] * gaps[2]
    def merge(even, odd):
        m = even.shape[0]
        r = dot(stacked(jnp.concatenate([even, odd], axis=1)), up_mat[...])
        return r[:m, :128] + (r[:m, 128:] + r[m:, :128])

    def climb(src, first, dst, to, count):
        x = src[pl.ds(first, 2 * count)].reshape(count, 2, 32, 128)
        u = merge(x[:, 0].reshape(count * 32, 128), x[:, 1].reshape(count * 32, 128))
        dst[pl.ds(to, count)] = u.reshape(count, 32, 128)

    for h in range(1, local + 1):
        count = leaf_dev >> h
        src, first = (wide_u, half) if h == 1 else (ulev, offsets[h - 1])
        csrc = wide_c if h == 1 else clev
        c = csrc[pl.ds(first, 2 * count)].reshape(count, 2, 8, 128)
        clev[pl.ds(offsets[h], count)] = (c[:, 0] + c[:, 1]) * 0.5
        step = min(count, 8)
        for j in range(0, count, step):
            climb(src, first + 2 * j, ulev, offsets[h] + j, step)

    root = offsets[local]
    if top:
        snd[0, 0:32] = ulev[root]
        snd[0, 32:40] = clev[root]
        rounds[0].start()

    def scale_of(h):
        return RADIUS * GROWTH**h

    for h in range(1, local):
        scale = scale_of(h)

        def couple_pair(p, scale=scale, base=offsets[h]):
            even = base + 2 * p
            gap = clev[even] - clev[even + 1]
            ends = jnp.concatenate([as_link(gap, units, scale), as_link(-gap, units, scale)], axis=1)
            shape = scale * scale * unit_gaps[...] + DELTA_SQ
            shapes = jnp.concatenate([shape, shape], axis=1)
            to_even, to_odd = tiles(unit_left[...], target_feats(ends), shapes)
            vlev[even] = fold(dot(stacked(ulev[even + 1]), to_even))
            vlev[even + 1] = fold(dot(stacked(ulev[even]), to_odd))

        pairs = leaf_dev >> (h + 1)
        unroll = min(pairs, 4)

        def pair_step(i, _, couple_pair=couple_pair, unroll=unroll):
            for k in range(unroll):
                couple_pair(i * unroll + k)
            return 0

        lax.fori_loop(0, pairs // unroll, pair_step, 0)

    def advance(b):
        rounds[b].wait()
        if b + 1 < top:
            mine, theirs = snd[b, 0:32], rcv[b, 0:32]
            low = bits[b] == 0
            u = merge(jnp.where(low, mine, theirs), jnp.where(low, theirs, mine))
            snd[b + 1, 0:32] = u
            snd[b + 1, 32:40] = (snd[b, 32:40] + rcv[b, 32:40]) * 0.5
            rounds[b + 1].start()

    if top:
        advance(0)

    shape0 = scale_of(0) * units - clev[root]

    def own_nodes(i, _):
        for k in range(8):
            l = i * 8 + k
            x = wide_c[half + l] + shape0
            node_s[half + l] = source_feats(as_source(x))
            node_t[l] = target_feats(as_target(x, 1.0))
            lanes = pl.ds(pl.multiple_of(l * 128, 128), 128)
            x = rows3(pos, lanes)
            near_s[half + l] = source_feats(as_source(x))
            near_t[l] = target_feats(as_target(x, 1.0))
            near_w[half + l] = stacked(chg[:, lanes])
        return 0

    lax.fori_loop(0, leaf_dev // 8, own_nodes, 0)
    if top > 1:
        advance(1)
    c_left.wait()
    c_right.wait()
    first_leaf = me * leaf_dev - half

    def far_leaf(l):
        total = None
        for s in range(0, far.shape[0], 2):
            i, j = ((far[t, l] - first_leaf) & (2 * leaf_dev - 1) for t in (s, s + 1))
            (g,) = tiles(jnp.concatenate([node_s[i], node_s[j]], axis=0), node_t[l])
            r = dot(jnp.concatenate([wide_w[i], wide_w[j]], axis=1), g)
            total = fold(r) if total is None else total + fold(r)
        vfar[l] = total

    def lower(v):
        m = v.shape[0]
        r = dot_nt(stacked(v), down_mat[...])
        both = r[:m, :256] + (r[:m, 256:] + r[m:, :256])
        return both[:, :128], both[:, 128:]

    def descend(v, dst, to):
        count = v.shape[0]
        lo, hi = lower(v.reshape(count * 32, 128))
        kids = jnp.stack([lo.reshape(count, 32, 128), hi.reshape(count, 32, 128)], axis=1)
        where = pl.ds(to, 2 * count)
        dst[where] = dst[where] + kids.reshape(2 * count, 32, 128)

    def inner():
        coupled = []
        for b in range(top):
            scale = scale_of(local + b)
            ends = as_link(snd[b, 32:40] - rcv[b, 32:40], units, scale)
            shape = scale * scale * unit_gaps[...] + DELTA_SQ
            (g,) = tiles(unit_left[...], target_feats(ends), shape)
            coupled.append(fold(dot(stacked(rcv[b, 0:32]), g)))
        field = jnp.zeros((32, 128), F32)
        for b in reversed(range(top)):
            lo, hi = lower(field)
            field = jnp.where(bits[b] == 0, lo, hi) + coupled[b]
        descend(field.reshape(1, 32, 128), vlev, offsets[local - 1])
        for h in range(local - 2, 0, -1):
            parents = leaf_dev >> (h + 1)
            step = min(parents, 8)
            for j in range(0, parents, step):
                descend(vlev[pl.ds(offsets[h + 1] + j, step)], vlev, offsets[h] + 2 * j)

    def far_group(g):
        def step(i, _):
            for k in range(4):
                far_leaf(g * group + i * 4 + k)
            return 0

        lax.fori_loop(0, group // 4, step, 0)

    b = 2
    pieces = list(halo)
    for k in range(chunks):
        u_left[k].wait()
        u_right[k].wait()
        if k + 2 < chunks:
            u_left[k + 2].start()
            u_right[k + 2].start()
        for side in (1, 2):
            got = cmsg[side]
            for m in range(group):
                j = half - (k + 1) * group + m if side == 1 else half + leaf_dev + k * group + m
                col = leaf_dev - (k + 1) * group + m if side == 1 else k * group + m
                c = jnp.broadcast_to(got[:, col : col + 1], (8, 128))
                node_s[j] = source_feats(as_source(c + shape0))
                wide_w[j] = stacked(wide_u[j])
        for g in (chunks - 1 - k, chunks + k):
            far_group(g)
            if b < top:
                advance(b)
                b += 1
            for copy in pieces[:2]:
                copy.start()
            pieces = pieces[2:]

    for copy in halo:
        copy.wait()
    wide = 2 * leaf_dev

    def near_halo(i, _):
        for k in range(4):
            j = i * 4 + k
            lanes = pl.ds(pl.multiple_of(j * 128, 128), 128)
            near_s[j] = source_feats(as_source(rows3(halo_pos_l, lanes)))
            near_w[j] = stacked(halo_chg_l[:, lanes])
            near_s[half + leaf_dev + j] = source_feats(as_source(rows3(halo_pos_r, lanes)))
            near_w[half + leaf_dev + j] = stacked(halo_chg_r[:, lanes])
        return 0

    lax.fori_loop(0, half // 4, near_halo, 0)
    near_s[wide] = source_feats(as_source(jnp.zeros((8, 128), F32)))
    near_w[wide] = jnp.zeros((64, 128), BF16)

    def near_leaf(l):
        total, used = None, used_slots[l]
        for s in range(0, near.shape[0], 2):
            i, j = (
                jnp.where(t < used, (near[t, l] - first_leaf) & (wide - 1), wide) for t in (s, s + 1)
            )
            (g,) = tiles(jnp.concatenate([near_s[i], near_s[j]], axis=0), near_t[l])
            r = dot(jnp.concatenate([near_w[i], near_w[j]], axis=1), g)
            total = fold(r) if total is None else total + fold(r)
        outs[:, pl.ds(pl.multiple_of(l * 128, 128), 128)] = total

    def near_step(i, _):
        for k in range(4):
            near_leaf(i * 4 + k)
        return 0

    lax.fori_loop(0, leaf_dev // 4 - 1, near_step, 0)
    while b < top:
        advance(b)
        b += 1
    inner()
    for m in range(leaf_dev - 4, leaf_dev):
        near_leaf(m)

    for j in range(0, half, 8):
        descend(vlev[pl.ds(offsets[1] + j, 8)], vfar, 2 * j)

    stores = []
    for i in range(parts // 2):
        for k in range(2 * group):
            l = i * 2 * group + k
            outs[:, pl.ds(l * 128, 128)] += fold(dot_nt(stacked(vfar[l]), stacked(bases[l])))
        lanes = pl.ds(i * 2 * span, 2 * span)
        stores.append(pltpu.make_async_copy(outs.at[:, lanes], out.at[:, lanes], store_sem.at[i]))
        stores[-1].start()
    for copy in stores:
        copy.wait()


def shards(n, positions, charges, bases, transfer, unit_nodes, near_list, near_count, far_list):
    leaf_dev = bases.shape[0]
    half, wide = leaf_dev // 2, 2 * leaf_dev
    top = n.bit_length() - 1
    smem = pl.BlockSpec(memory_space=pltpu.SMEM)
    hbm = pl.BlockSpec(memory_space=pltpu.HBM)
    span = half * 128
    shape = jax.ShapeDtypeStruct
    return pl.pallas_call(
        functools.partial(tree_kernel, n),
        out_shape=shape((32, leaf_dev * 128), F32),
        in_specs=[hbm] * 5 + [smem] * 3,
        out_specs=hbm,
        scratch_shapes=[
            pltpu.VMEM((3, span), F32),
            pltpu.VMEM((3, span), F32),
            pltpu.VMEM((32, span), F32),
            pltpu.VMEM((32, span), F32),
            pltpu.VMEM((wide + 1, 128, FEATS), BF16),
            pltpu.VMEM((leaf_dev, FEATS, 128), BF16),
            pltpu.VMEM((wide + 1, 64, 128), BF16),
            pltpu.VMEM((3, leaf_dev * 128), F32),
            pltpu.VMEM((32, leaf_dev * 128), F32),
            pltpu.VMEM((leaf_dev, 128, 128), F32),
            pltpu.VMEM((2, 128, 128), F32),
            pltpu.VMEM((3, 128), F32),
            pltpu.VMEM((wide, 32, 128), F32),
            pltpu.VMEM((wide, 64, 128), BF16),
            pltpu.VMEM((wide, 8, 128), F32),
            pltpu.VMEM((leaf_dev, 32, 128), F32),
            pltpu.VMEM((leaf_dev, 8, 128), F32),
            pltpu.VMEM((leaf_dev, 32, 128), F32),
            pltpu.VMEM((leaf_dev, 32, 128), F32),
            pltpu.VMEM((256, 256), BF16),
            pltpu.VMEM((512, 128), BF16),
            pltpu.VMEM((128, FEATS), BF16),
            pltpu.VMEM((128, 128), F32),
            pltpu.VMEM((wide, 128, FEATS), BF16),
            pltpu.VMEM((leaf_dev, FEATS, 128), BF16),
            pltpu.VMEM((3, 8, 128), F32),
            pltpu.VMEM((max(top, 1), 40, 128), F32),
            pltpu.VMEM((max(top, 1), 40, 128), F32),
            pltpu.VMEM((32, leaf_dev * 128), F32),
            pltpu.SemaphoreType.DMA((leaf_dev // 4 + 4 + top,)),
            pltpu.SemaphoreType.DMA((leaf_dev // 4 + 4 + top,)),
            pltpu.SemaphoreType.DMA((4 + leaf_dev // 8,)),
            pltpu.SemaphoreType.DMA((leaf_dev // 16,)),
        ],
        compiler_params=pltpu.CompilerParams(
            collective_id=0, has_side_effects=True, vmem_limit_bytes=56 << 20
        ),
        name="h2",
    )(positions, charges, bases, transfer, unit_nodes, far_list.T, near_list.T, near_count)


def solution(mesh):
    placed = (
        P(None, "leaf"),
        P(None, "leaf"),
        P("leaf", None, None),
        P(),
        P(),
        P("leaf", None),
        P("leaf"),
        P("leaf", None),
    )
    return jax.shard_map(
        functools.partial(shards, mesh.shape["leaf"]),
        mesh=mesh,
        in_specs=placed,
        out_specs=P(None, "leaf"),
        check_vma=False,
    )
```

```python
import functools

import jax
import jax.numpy as jnp
from jax import lax
from jax.experimental import pallas as pl
from jax.experimental.pallas import tpu as pltpu
from jax.sharding import PartitionSpec as P

DELTA_SQ = 0.0625
RADIUS = 0.4
GROWTH = 1.26
F32, BF16 = jnp.float32, jnp.bfloat16
MESH = pl.DeviceIdType.MESH
NT = (((1,), (1,)), ((), ()))
FEATS = 48


def dot(a, b):
    return jnp.dot(a, b, preferred_element_type=F32)


def dot_nt(a, b):
    return lax.dot_general(a, b, NT, preferred_element_type=F32)


def halves(x):
    hi = x.astype(BF16)
    return hi, (x - hi.astype(F32)).astype(BF16)


def thirds(x):
    a = x.astype(BF16).astype(F32)
    rest = x - a
    b = rest.astype(BF16).astype(F32)
    return a, b, rest - b


def stacked(x):
    hi, lo = halves(x)
    return jnp.concatenate([hi, lo], axis=0)


def target_feats(y):
    a, b, c = thirds(y)
    return jnp.concatenate([a, a, a, b, b, c], axis=0).astype(BF16)


def source_feats(x):
    a, b, c = thirds(x)
    return jnp.concatenate([a, b, c, a, b, a], axis=0).T.astype(BF16)


def row_ids():
    return lax.broadcasted_iota(jnp.int32, (8, 128), 0)


def rows3(ref, lanes):
    rows = row_ids()
    x = jnp.where(rows == 0, ref[0:1, lanes], 0.0)
    x = jnp.where(rows == 1, ref[1:2, lanes], x)
    return jnp.where(rows == 2, ref[2:3, lanes], x)


def as_source(x):
    rows = row_ids()
    norm = jnp.sum(x * x, axis=0, keepdims=True)
    return jnp.where(rows == 3, 1.0, jnp.where(rows == 4, norm, -2.0 * x))


def as_target(y, scale):
    rows = row_ids()
    norm = jnp.sum(y * y, axis=0, keepdims=True)
    return jnp.where(rows == 3, norm + DELTA_SQ, jnp.where(rows == 4, scale * scale, scale * y))


def as_link(gap, units, scale):
    rest = jnp.sum(gap * (gap + (2.0 * scale) * units), axis=0, keepdims=True)
    return jnp.where(row_ids() == 3, rest, scale * gap)


def fold(r):
    m, n = r.shape[0] // 2, r.shape[1] // 2
    return r[:m, :n] + (r[:m, n:] + r[m:, :n]) + r[m:, n:]


def tiles(left, right, extra=None):
    dist_sq = dot(left, right)
    hi, lo = halves(lax.rsqrt(dist_sq if extra is None else dist_sq + extra))
    return [
        jnp.concatenate([hi[:, i : i + 128], lo[:, i : i + 128]], axis=1)
        for i in range(0, right.shape[1], 128)
    ]


def tree_kernel(
    n,
    pos_in,
    chg_in,
    bases_in,
    transfer_in,
    unit_in,
    far,
    near,
    used_slots,
    out,
    halo_pos_l,
    halo_pos_r,
    halo_chg_l,
    halo_chg_r,
    near_s,
    near_t,
    near_w,
    pos,
    chg,
    bases,
    transfer,
    unit,
    wide_u,
    wide_w,
    wide_c,
    ulev,
    clev,
    vlev,
    vfar,
    up_mat,
    down_mat,
    unit_left,
    unit_gaps,
    node_s,
    node_t,
    cmsg,
    snd,
    rcv,
    outs,
    send_sem,
    recv_sem,
    load_sem,
    store_sem,
):
    me = lax.axis_index("leaf")
    leaf_dev = bases_in.shape[0]
    half = leaf_dev // 2
    local = leaf_dev.bit_length() - 1
    top = n.bit_length() - 1
    left, right = lax.rem(me + n - 1, n), lax.rem(me + 1, n)
    bits = [(me // (1 << b)) % 2 for b in range(top)]
    partners = [me + (1 << b) * (1 - 2 * bits[b]) for b in range(top)]
    offsets = [0] * (local + 1)
    for h in range(2, local + 1):
        offsets[h] = offsets[h - 1] + (leaf_dev >> (h - 1))

    group = 8
    parts = leaf_dev // group
    order = [j for k in range(parts // 2) for j in (k, parts - 1 - k)]
    loads = [
        pltpu.make_async_copy(src, dst, load_sem.at[i])
        for i, (src, dst) in enumerate(
            [(chg_in, chg), (pos_in, pos), (transfer_in, transfer), (unit_in, unit)]
            + [(bases_in.at[pl.ds(j * group, group)], bases.at[pl.ds(j * group, group)]) for j in order]
        )
    ]
    for copy in loads[:2] + loads[4:] + loads[2:4]:
        copy.start()
    barrier = pltpu.get_barrier_semaphore()
    for other in [left, right] + partners:
        pl.semaphore_signal(barrier, inc=1, device_id=(other,), device_id_type=MESH)

    def remote(src, dst, which, device):
        return pltpu.make_async_remote_copy(
            src_ref=src,
            dst_ref=dst,
            send_sem=send_sem.at[which],
            recv_sem=recv_sem.at[which],
            device_id=(device,),
            device_id_type=MESH,
        )

    chunks = parts // 2
    u_left, u_right = [], []
    for k in range(chunks):
        src, dst = half + k * group, half + leaf_dev + k * group
        u_left.append(remote(wide_u.at[pl.ds(src, group)], wide_u.at[pl.ds(dst, group)], k, left))
        src, dst = half + leaf_dev - (k + 1) * group, half - (k + 1) * group
        u_right.append(
            remote(wide_u.at[pl.ds(src, group)], wide_u.at[pl.ds(dst, group)], chunks + k, right)
        )
    at = 2 * chunks
    c_left = remote(cmsg.at[0], cmsg.at[2], at, left)
    c_right = remote(cmsg.at[0], cmsg.at[1], at + 1, right)
    span = group * 128
    halo = [
        remote(pos_in.at[:, pl.ds(0, half * 128)], halo_pos_r, at + 2, left),
        remote(pos_in.at[:, pl.ds(half * 128, half * 128)], halo_pos_l, at + 3, right),
    ]
    for k in range(chunks):
        lanes = pl.ds(k * span, span)
        halo.append(remote(chg.at[:, lanes], halo_chg_r.at[:, lanes], at + 4 + k, left))
        mine = pl.ds(half * 128 + k * span, span)
        halo.append(remote(chg.at[:, mine], halo_chg_l.at[:, lanes], at + 4 + chunks + k, right))
    at = at + 4 + 2 * chunks
    rounds = [remote(snd.at[b], rcv.at[b], at + b, partners[b]) for b in range(top)]

    lanes_id = lax.broadcasted_iota(jnp.int32, (8, 128), 1)

    def leaf_group(i, cols):
        loads[4 + order.index(i)].wait()
        for k in range(group):
            l = i * group + k
            span_l = pl.ds(l * 128, 128)
            hi, lo = halves(bases[l])
            u = fold(dot(stacked(chg[:, span_l]), jnp.concatenate([hi, lo], axis=1)))
            wide_u[half + l] = u
            wide_w[half + l] = stacked(u)
            center = jnp.sum(rows3(pos, span_l), axis=1, keepdims=True) * (1.0 / 128)
            wide_c[half + l] = jnp.broadcast_to(center, (8, 128))
            cols = jnp.where(lanes_id == l, center, cols)
        return cols

    cols = jnp.zeros((8, 128), F32)
    for copy in loads[:2]:
        copy.wait()
    for k in range(chunks):
        cols = leaf_group(k, cols)
        cols = leaf_group(parts - 1 - k, cols)
    cmsg[0] = cols
    for copy in loads[2:4]:
        copy.wait()

    t0, t1 = transfer[0], transfer[1]
    h0, l0 = halves(t0)
    h1, l1 = halves(t1)
    up_mat[...] = jnp.concatenate(
        [jnp.concatenate([h0, l0], axis=1), jnp.concatenate([h1, l1], axis=1)], axis=0
    )
    down_mat[...] = jnp.concatenate([h0, h1, l0, l1], axis=0)
    units = rows3(unit, slice(None))
    unit_left[...] = source_feats(as_source(units))
    columns = units.T
    gaps = [columns[:, c : c + 1] - units[c : c + 1, :] for c in range(3)]
    unit_gaps[...] = gaps[0] * gaps[0] + gaps[1] * gaps[1] + gaps[2] * gaps[2]
    def merge(even, odd):
        m = even.shape[0]
        r = dot(stacked(jnp.concatenate([even, odd], axis=1)), up_mat[...])
        return r[:m, :128] + (r[:m, 128:] + r[m:, :128])

    def climb(src, first, dst, to, count):
        x = src[pl.ds(first, 2 * count)].reshape(count, 2, 32, 128)
        u = merge(x[:, 0].reshape(count * 32, 128), x[:, 1].reshape(count * 32, 128))
        dst[pl.ds(to, count)] = u.reshape(count, 32, 128)

    for h in range(1, local + 1):
        count = leaf_dev >> h
        src, first = (wide_u, half) if h == 1 else (ulev, offsets[h - 1])
        csrc = wide_c if h == 1 else clev
        c = csrc[pl.ds(first, 2 * count)].reshape(count, 2, 8, 128)
        clev[pl.ds(offsets[h], count)] = (c[:, 0] + c[:, 1]) * 0.5
        step = min(count, 8)
        for j in range(0, count, step):
            climb(src, first + 2 * j, ulev, offsets[h] + j, step)

    root = offsets[local]
    snd[0, 0:32] = ulev[root]
    snd[0, 32:40] = clev[root]

    def scale_of(h):
        return RADIUS * GROWTH**h

    shape0 = scale_of(0) * units - clev[root]

    def own_nodes(i, _):
        for k in range(8):
            l = i * 8 + k
            x = wide_c[half + l] + shape0
            node_s[half + l] = source_feats(as_source(x))
            node_t[l] = target_feats(as_target(x, 1.0))
            lanes = pl.ds(pl.multiple_of(l * 128, 128), 128)
            x = rows3(pos, lanes)
            near_s[half + l] = source_feats(as_source(x))
            near_t[l] = target_feats(as_target(x, 1.0))
            near_w[half + l] = stacked(chg[:, lanes])
        return 0

    lax.fori_loop(0, leaf_dev // 8, own_nodes, 0)
    pl.semaphore_wait(barrier, top + 2)
    if top:
        rounds[0].start()
    c_left.start()
    c_right.start()
    for k in range(2):
        u_left[k].start()
        u_right[k].start()

    for h in range(1, local):
        scale = scale_of(h)

        def couple_pair(p, scale=scale, base=offsets[h]):
            even = base + 2 * p
            gap = clev[even] - clev[even + 1]
            ends = jnp.concatenate([as_link(gap, units, scale), as_link(-gap, units, scale)], axis=1)
            shape = scale * scale * unit_gaps[...] + DELTA_SQ
            shapes = jnp.concatenate([shape, shape], axis=1)
            to_even, to_odd = tiles(unit_left[...], target_feats(ends), shapes)
            vlev[even] = fold(dot(stacked(ulev[even + 1]), to_even))
            vlev[even + 1] = fold(dot(stacked(ulev[even]), to_odd))

        pairs = leaf_dev >> (h + 1)
        unroll = min(pairs, 4)

        def pair_step(i, _, couple_pair=couple_pair, unroll=unroll):
            for k in range(unroll):
                couple_pair(i * unroll + k)
            return 0

        lax.fori_loop(0, pairs // unroll, pair_step, 0)

    def advance(b):
        rounds[b].wait()
        if b + 1 < top:
            mine, theirs = snd[b, 0:32], rcv[b, 0:32]
            low = bits[b] == 0
            u = merge(jnp.where(low, mine, theirs), jnp.where(low, theirs, mine))
            snd[b + 1, 0:32] = u
            snd[b + 1, 32:40] = (snd[b, 32:40] + rcv[b, 32:40]) * 0.5
            rounds[b + 1].start()

    if top:
        advance(0)

    if top > 1:
        advance(1)
    c_left.wait()
    c_right.wait()
    first_leaf = me * leaf_dev - half

    def far_leaf(l):
        total = None
        for s in range(0, far.shape[0], 2):
            i, j = ((far[t, l] - first_leaf) & (2 * leaf_dev - 1) for t in (s, s + 1))
            (g,) = tiles(jnp.concatenate([node_s[i], node_s[j]], axis=0), node_t[l])
            r = dot(jnp.concatenate([wide_w[i], wide_w[j]], axis=1), g)
            total = fold(r) if total is None else total + fold(r)
        vfar[l] = total

    def lower(v):
        m = v.shape[0]
        r = dot_nt(stacked(v), down_mat[...])
        both = r[:m, :256] + (r[:m, 256:] + r[m:, :256])
        return both[:, :128], both[:, 128:]

    def descend(v, dst, to):
        count = v.shape[0]
        lo, hi = lower(v.reshape(count * 32, 128))
        kids = jnp.stack([lo.reshape(count, 32, 128), hi.reshape(count, 32, 128)], axis=1)
        where = pl.ds(to, 2 * count)
        dst[where] = dst[where] + kids.reshape(2 * count, 32, 128)

    def inner():
        coupled = []
        for b in range(top):
            scale = scale_of(local + b)
            ends = as_link(snd[b, 32:40] - rcv[b, 32:40], units, scale)
            shape = scale * scale * unit_gaps[...] + DELTA_SQ
            (g,) = tiles(unit_left[...], target_feats(ends), shape)
            coupled.append(fold(dot(stacked(rcv[b, 0:32]), g)))
        field = jnp.zeros((32, 128), F32)
        for b in reversed(range(top)):
            lo, hi = lower(field)
            field = jnp.where(bits[b] == 0, lo, hi) + coupled[b]
        descend(field.reshape(1, 32, 128), vlev, offsets[local - 1])
        for h in range(local - 2, 0, -1):
            parents = leaf_dev >> (h + 1)
            step = min(parents, 8)
            for j in range(0, parents, step):
                descend(vlev[pl.ds(offsets[h + 1] + j, step)], vlev, offsets[h] + 2 * j)

    def far_group(g):
        def step(i, _):
            for k in range(4):
                far_leaf(g * group + i * 4 + k)
            return 0

        lax.fori_loop(0, group // 4, step, 0)

    b = 2
    pieces = list(halo)
    for k in range(chunks):
        u_left[k].wait()
        u_right[k].wait()
        if k + 2 < chunks:
            u_left[k + 2].start()
            u_right[k + 2].start()
        for side in (1, 2):
            got = cmsg[side]
            for m in range(group):
                j = half - (k + 1) * group + m if side == 1 else half + leaf_dev + k * group + m
                col = leaf_dev - (k + 1) * group + m if side == 1 else k * group + m
                c = jnp.broadcast_to(got[:, col : col + 1], (8, 128))
                node_s[j] = source_feats(as_source(c + shape0))
                wide_w[j] = stacked(wide_u[j])
        for g in (chunks - 1 - k, chunks + k):
            far_group(g)
            if b < top:
                advance(b)
                b += 1
            for copy in pieces[:2]:
                copy.start()
            pieces = pieces[2:]

    for copy in halo:
        copy.wait()
    wide = 2 * leaf_dev

    def near_halo(i, _):
        for k in range(4):
            j = i * 4 + k
            lanes = pl.ds(pl.multiple_of(j * 128, 128), 128)
            near_s[j] = source_feats(as_source(rows3(halo_pos_l, lanes)))
            near_w[j] = stacked(halo_chg_l[:, lanes])
            near_s[half + leaf_dev + j] = source_feats(as_source(rows3(halo_pos_r, lanes)))
            near_w[half + leaf_dev + j] = stacked(halo_chg_r[:, lanes])
        return 0

    lax.fori_loop(0, half // 4, near_halo, 0)
    near_s[wide] = source_feats(as_source(jnp.zeros((8, 128), F32)))
    near_w[wide] = jnp.zeros((64, 128), BF16)

    def near_leaf(l):
        total, used = None, used_slots[l]
        for s in range(0, near.shape[0], 2):
            i, j = (
                jnp.where(t < used, (near[t, l] - first_leaf) & (wide - 1), wide) for t in (s, s + 1)
            )
            (g,) = tiles(jnp.concatenate([near_s[i], near_s[j]], axis=0), near_t[l])
            r = dot(jnp.concatenate([near_w[i], near_w[j]], axis=1), g)
            total = fold(r) if total is None else total + fold(r)
        outs[:, pl.ds(pl.multiple_of(l * 128, 128), 128)] = total

    def near_step(i, _):
        for k in range(4):
            near_leaf(i * 4 + k)
        return 0

    lax.fori_loop(0, leaf_dev // 4 - 1, near_step, 0)
    while b < top:
        advance(b)
        b += 1
    inner()
    for m in range(leaf_dev - 4, leaf_dev):
        near_leaf(m)

    for j in range(0, half, 8):
        descend(vlev[pl.ds(offsets[1] + j, 8)], vfar, 2 * j)

    stores = []
    for i in range(parts // 2):
        for k in range(2 * group):
            l = i * 2 * group + k
            outs[:, pl.ds(l * 128, 128)] += fold(dot_nt(stacked(vfar[l]), stacked(bases[l])))
        lanes = pl.ds(i * 2 * span, 2 * span)
        stores.append(pltpu.make_async_copy(outs.at[:, lanes], out.at[:, lanes], store_sem.at[i]))
        stores[-1].start()
    for copy in stores:
        copy.wait()


def shards(n, positions, charges, bases, transfer, unit_nodes, near_list, near_count, far_list):
    leaf_dev = bases.shape[0]
    half, wide = leaf_dev // 2, 2 * leaf_dev
    top = n.bit_length() - 1
    smem = pl.BlockSpec(memory_space=pltpu.SMEM)
    hbm = pl.BlockSpec(memory_space=pltpu.HBM)
    span = half * 128
    shape = jax.ShapeDtypeStruct
    return pl.pallas_call(
        functools.partial(tree_kernel, n),
        out_shape=shape((32, leaf_dev * 128), F32),
        in_specs=[hbm] * 5 + [smem] * 3,
        out_specs=hbm,
        scratch_shapes=[
            pltpu.VMEM((3, span), F32),
            pltpu.VMEM((3, span), F32),
            pltpu.VMEM((32, span), F32),
            pltpu.VMEM((32, span), F32),
            pltpu.VMEM((wide + 1, 128, FEATS), BF16),
            pltpu.VMEM((leaf_dev, FEATS, 128), BF16),
            pltpu.VMEM((wide + 1, 64, 128), BF16),
            pltpu.VMEM((3, leaf_dev * 128), F32),
            pltpu.VMEM((32, leaf_dev * 128), F32),
            pltpu.VMEM((leaf_dev, 128, 128), F32),
            pltpu.VMEM((2, 128, 128), F32),
            pltpu.VMEM((3, 128), F32),
            pltpu.VMEM((wide, 32, 128), F32),
            pltpu.VMEM((wide, 64, 128), BF16),
            pltpu.VMEM((wide, 8, 128), F32),
            pltpu.VMEM((leaf_dev, 32, 128), F32),
            pltpu.VMEM((leaf_dev, 8, 128), F32),
            pltpu.VMEM((leaf_dev, 32, 128), F32),
            pltpu.VMEM((leaf_dev, 32, 128), F32),
            pltpu.VMEM((256, 256), BF16),
            pltpu.VMEM((512, 128), BF16),
            pltpu.VMEM((128, FEATS), BF16),
            pltpu.VMEM((128, 128), F32),
            pltpu.VMEM((wide, 128, FEATS), BF16),
            pltpu.VMEM((leaf_dev, FEATS, 128), BF16),
            pltpu.VMEM((3, 8, 128), F32),
            pltpu.VMEM((max(top, 1), 40, 128), F32),
            pltpu.VMEM((max(top, 1), 40, 128), F32),
            pltpu.VMEM((32, leaf_dev * 128), F32),
            pltpu.SemaphoreType.DMA((leaf_dev // 4 + 4 + top,)),
            pltpu.SemaphoreType.DMA((leaf_dev // 4 + 4 + top,)),
            pltpu.SemaphoreType.DMA((4 + leaf_dev // 8,)),
            pltpu.SemaphoreType.DMA((leaf_dev // 16,)),
        ],
        compiler_params=pltpu.CompilerParams(
            collective_id=0, has_side_effects=True, vmem_limit_bytes=56 << 20
        ),
        name="h2",
    )(positions, charges, bases, transfer, unit_nodes, far_list.T, near_list.T, near_count)


def solution(mesh):
    placed = (
        P(None, "leaf"),
        P(None, "leaf"),
        P("leaf", None, None),
        P(),
        P(),
        P("leaf", None),
        P("leaf"),
        P("leaf", None),
    )
    return jax.shard_map(
        functools.partial(shards, mesh.shape["leaf"]),
        mesh=mesh,
        in_specs=placed,
        out_specs=P(None, "leaf"),
        check_vma=False,
    )
```
